32 devices in a mesh: dp: 8 (over y, x, core), proto: 4 (over z).
Axes of the slice: x: 2, y: 2, z: 4, core: 2. Of those that a mesh axis runs over, the one named last changes fastest.
Arguments:
- student_feats: float32 [1280, 256], P('dp'), may hold values from -6 to 6
- teacher_feats: float32 [256, 256], P('dp'), may hold values from -6 to 6
- student_proto: float32 [256, 32768], P('dp', 'proto'), may hold values from -6 to 6
- teacher_proto: float32 [256, 32768], P('dp', 'proto'), may hold values from -6 to 6
- crops: int32 [1280, 2], P('dp'), may hold values from 0 to 15, as said below
- step: int32 [1], replicated, may hold values from 0 to 24999
Outputs:
- student_next: float32 [256, 32768], P('dp', 'proto')
- teacher_next: float32 [256, 32768], P('dp', 'proto')
- feature_grad: float32 [1280, 256], P('dp')
The draws below stay inside these ranges and needn't reach their ends.
Inputs may be any that keep to these rules, and one draw needn't show every extreme that they name: Within each device's block of 160 rows every pair (image i < 16, slot c < 10) appears exactly once; slots below 2 are the global crops, slot g of image i being the same crop as teacher row 2 * i + g of that block.
All inputs are finite; a program needn't handle non-finite values.
Results may differ from the reference program's by a relative error of at most 0.0003.
Values sent between devices are 32-bit elements; how exact they have to be, the bound alone decides.
A program may use at most 128 MiB of HBM per device.

```python
import jax
import jax.numpy as jnp
from jax import lax

D = 256
IMG_DEV = 16
CROPS = 10
GLOBAL_CROPS = 2
ITERS = 3
WARM_STEPS = 12500
TOTAL_STEPS = 625000
IMAGES = 128
SROWS = 1280
TROWS = 256
PROTOS = 32768
N_DP = 8


def draw_crops(key, part):
    per_rows = CROPS * IMG_DEV
    blocks = SROWS // per_rows
    keys = jax.random.split(jax.random.fold_in(key, 17), blocks)
    orders = jax.vmap(lambda one: jax.random.permutation(one, per_rows))(keys)
    flat = orders.reshape(-1).astype(jnp.int32)
    return jnp.stack([flat // CROPS, flat % CROPS], axis=1).astype(jnp.int32)


def block_levels(own_key, dims, shards, low, top_value):
    loudness, own = 1.0, jax.random.fold_in(own_key, 6)
    for axis_at, shards_of in shards:
        heights = jnp.exp(jax.random.uniform(jax.random.fold_in(own, axis_at), (shards_of,), jnp.float32, low / len(shards), top_value / len(shards)))
        loudness = loudness * jnp.repeat(heights, dims[axis_at] // shards_of).reshape([-1 if axis == axis_at else 1 for axis in range(len(dims))])
    return loudness


def centred(stream_key, extent, scale, most, cuts=(), held_as=jnp.bfloat16):
    entries = scale * jax.random.normal(stream_key, extent, jnp.float32)
    if cuts:
        entries = entries * block_levels(stream_key, extent, cuts, -0.22, 0.18)
    return jnp.clip(entries, -most, most).astype(held_as)


def setup_inputs(seed: int = 0) -> dict:
    key_of = jax.random.split(jax.random.key(seed), 7)
    student_feats = centred(key_of[0], (SROWS, D), 1.0, 6.0, ((0, 8),), jnp.float32)
    teacher_feats = centred(key_of[1], (TROWS, D), 1.0, 6.0, ((0, 8),), jnp.float32)
    student_proto = centred(key_of[2], (D, PROTOS), 1.0, 6.0, ((0, 8), (1, 4)), jnp.float32)
    teacher_proto = centred(key_of[3], (D, PROTOS), 1.0, 6.0, ((0, 8), (1, 4)), jnp.float32)
    crops = draw_crops(jax.random.fold_in(key_of[6], 71), 0)
    step = jax.random.randint(key_of[5], (1,), 0, 2 * WARM_STEPS).astype(jnp.int32)
    return {"student_feats": student_feats, "teacher_feats": teacher_feats, "student_proto": student_proto, "teacher_proto": teacher_proto, "crops": crops, "step": step}


student_temp = 0.1
loss_scale = 16777216.0
norm_eps = 1e-06
square_eps = 1e-06
rate_peak = 0.05
weight_decay = 0.04
momentum_base = 0.994
highest = lax.Precision.HIGHEST

def plan(step):
    value = step[0].astype(jnp.float32)
    ramp = jnp.minimum(1.0, value / WARM_STEPS)
    rate = rate_peak * (0.25 + 0.75 * ramp)
    teacher_temp = 0.04 + 0.03 * ramp
    momentum = 1.0 - (1.0 - momentum_base) * (jnp.cos(jnp.pi * value / TOTAL_STEPS) + 1.0) * 0.5
    return (rate, teacher_temp, momentum)

def unit_rows(values):
    norm = jnp.sqrt(lax.optimization_barrier(jnp.sum(values * values, axis=1, keepdims=True)) + norm_eps)
    return (values / norm, norm)

def unit_columns(values):
    norm = jnp.sqrt(lax.optimization_barrier(jnp.sum(values * values, axis=0, keepdims=True)) + norm_eps)
    return (values / norm, norm)

def reference(student_feats, teacher_feats, student_proto, teacher_proto, crops, step):
    rate, teacher_temp, momentum = plan(step)
    student_unit, student_norm = unit_columns(student_proto)
    teacher_unit, teacher_norm = unit_columns(teacher_proto)
    t_unit, t_norm = unit_rows(teacher_feats)
    assign = jnp.exp(jnp.dot(t_unit, teacher_unit, precision=highest, preferred_element_type=jnp.float32) / teacher_temp)
    for turn in range(ITERS):
        assign = assign / lax.optimization_barrier(jnp.sum(assign, axis=0, keepdims=True))
        assign = assign / lax.optimization_barrier(jnp.sum(assign, axis=1, keepdims=True))
    s_unit, s_norm = unit_rows(student_feats)
    pair_total = GLOBAL_CROPS * (GLOBAL_CROPS - 1) + (CROPS - GLOBAL_CROPS) * GLOBAL_CROPS
    coef = loss_scale / (pair_total * IMAGES * student_temp)
    per_rows = CROPS * IMG_DEV
    per_teach = GLOBAL_CROPS * IMG_DEV
    row_blocks = s_unit.reshape(N_DP, per_rows, D)
    table_blocks = crops.reshape(N_DP, per_rows, 2)
    assign_blocks = assign.reshape(N_DP, per_teach, PROTOS)
    teach_iota = lax.broadcasted_iota(jnp.int32, (1, per_teach), 1)

    def per_device(carry, pieces):
        rows, table, local_assign = pieces
        logits = jnp.dot(rows, student_unit, precision=highest, preferred_element_type=jnp.float32) / student_temp
        expo = jnp.exp(logits)
        prob = expo / lax.optimization_barrier(jnp.sum(expo, axis=1, keepdims=True))
        same = table[:, 0:1] == teach_iota // GLOBAL_CROPS
        other = table[:, 1:2] != teach_iota % GLOBAL_CROPS
        pairs = jnp.where(same & other, 1.0, 0.0).astype(jnp.float32)
        target = jnp.dot(pairs, local_assign, precision=highest, preferred_element_type=jnp.float32)
        count = lax.optimization_barrier(jnp.sum(pairs, axis=1, keepdims=True))
        dscore = coef * (count * prob - target)
        carry = carry + jnp.dot(rows.T, dscore, precision=highest, preferred_element_type=jnp.float32)
        back = jnp.dot(dscore, student_unit.T, precision=highest, preferred_element_type=jnp.float32)
        return (carry, back)
    grad_unit, backs = lax.scan(per_device, jnp.zeros((D, PROTOS), jnp.float32), (row_blocks, table_blocks, assign_blocks))
    feature_unit = backs.reshape(SROWS, D)
    feature_grad = (feature_unit - s_unit * lax.optimization_barrier(jnp.sum(s_unit * feature_unit, axis=1, keepdims=True))) / s_norm
    along = lax.optimization_barrier(jnp.sum(student_unit * grad_unit, axis=0, keepdims=True))
    proto_grad = (grad_unit - student_unit * along) / student_norm
    square = lax.optimization_barrier(jnp.mean(proto_grad * proto_grad, axis=0, keepdims=True))
    direction = proto_grad / jnp.sqrt(square + square_eps)
    student_next = student_proto - rate * (direction + weight_decay * student_proto)
    teacher_next = momentum * teacher_proto + (1.0 - momentum) * student_next
    return (student_next, teacher_next, feature_grad)
```

```python
import jax
import jax.numpy as jnp
from jax import lax
from jax.sharding import PartitionSpec as P

CROPS = 10
GLOBAL_CROPS = 2
ITERS = 3
WARM_STEPS = 12500
TOTAL_STEPS = 625000


student_temp = 0.1
loss_scale = 16777216.0
norm_eps = 1e-06
square_eps = 1e-06
rate_peak = 0.05
weight_decay = 0.04
momentum_base = 0.994
highest = lax.Precision.HIGHEST


def plan(step):
    value = step[0].astype(jnp.float32)
    ramp = jnp.minimum(1.0, value / WARM_STEPS)
    rate = rate_peak * (0.25 + 0.75 * ramp)
    teacher_temp = 0.04 + 0.03 * ramp
    momentum = 1.0 - (1.0 - momentum_base) * (jnp.cos(jnp.pi * value / TOTAL_STEPS) + 1.0) * 0.5
    return (rate, teacher_temp, momentum)


def unit_rows(values):
    norm = jnp.sqrt(jnp.sum(values * values, axis=1, keepdims=True) + norm_eps)
    return (values / norm, norm)


def unit_columns(values):
    norm = jnp.sqrt(jnp.sum(values * values, axis=0, keepdims=True) + norm_eps)
    return (values / norm, norm)


def dot(left, right, dims):
    return lax.dot_general(
        left, right, (dims, ((), ())), precision=highest, preferred_element_type=jnp.float32
    )


def body(student_feats, teacher_feats, student_proto, teacher_proto, crops, step):
    rate, teacher_temp, momentum = plan(step)
    parts = lax.axis_size("dp")
    t_unit, t_norm = unit_rows(teacher_feats)
    s_unit, s_norm = unit_rows(student_feats)
    crop_rows, width = s_unit.shape
    teach_rows = t_unit.shape[0]
    own_rows, columns = student_proto.shape
    share = columns // parts
    images = teach_rows // GLOBAL_CROPS * parts
    pair_total = GLOBAL_CROPS * (GLOBAL_CROPS - 1) + (CROPS - GLOBAL_CROPS) * GLOBAL_CROPS
    coef = loss_scale / (pair_total * images * student_temp)
    teach_iota = lax.broadcasted_iota(jnp.int32, (1, teach_rows), 1)
    same = crops[:, 0:1] == teach_iota // GLOBAL_CROPS
    other = crops[:, 1:2] != teach_iota % GLOBAL_CROPS
    pairs = jnp.where(same & other, 1.0, 0.0).astype(jnp.float32)
    count = jnp.sum(pairs, axis=1, keepdims=True)
    mixed = dot(pairs, s_unit, ((0,), (0,)))
    count_rows = jnp.pad(count.reshape(1, crop_rows), ((0, 0), (0, -crop_rows % width)))
    count_rows = count_rows.reshape(-1, width)
    packed = jnp.concatenate([s_unit, t_unit, mixed, count_rows], axis=0)
    packed = lax.all_gather(packed, "dp", axis=0, tiled=False)
    protos = jnp.stack([student_proto, teacher_proto])
    protos = lax.all_to_all(protos, "dp", split_axis=2, concat_axis=1, tiled=True)
    one, two = crop_rows, crop_rows + teach_rows
    three = two + teach_rows
    all_s = packed[:, :one].reshape(parts * crop_rows, width)
    all_t = packed[:, one:two].reshape(parts * teach_rows, width)
    all_mixed = packed[:, two:three].reshape(parts * teach_rows, width)
    all_count = packed[:, three:].reshape(parts, -1)[:, :crop_rows].reshape(-1, 1)
    student_cols = protos[0]
    student_unit, student_norm = unit_columns(student_cols)
    teacher_unit, teacher_norm = unit_columns(protos[1])
    both = ("dp", "proto")
    assign = jnp.exp(dot(all_t, teacher_unit, ((1,), (0,))) / teacher_temp)
    expo = jnp.exp(dot(all_s, student_unit, ((1,), (0,))) / student_temp)
    total = jnp.sum(expo, axis=1)
    for turn in range(ITERS):
        assign = assign / jnp.sum(assign, axis=0, keepdims=True)
        row = jnp.sum(assign, axis=1)
        if turn == 0:
            row, total = lax.psum((row, total), both)
        else:
            row = lax.psum(row, both)
        assign = assign / row[:, None]
    total = total[:, None]
    back = dot(expo, student_unit, ((1,), (1,))).reshape(parts, crop_rows, width)
    back_target = dot(assign, student_unit, ((1,), (1,))).reshape(parts, teach_rows, width)
    sums = lax.psum_scatter(
        jnp.concatenate([back, back_target], axis=1), "dp", scatter_dimension=0, tiled=False
    )
    sums = lax.psum(sums, "proto")
    own_total = lax.dynamic_slice_in_dim(total, lax.axis_index("dp") * crop_rows, crop_rows, 0)
    feature_unit = coef * (
        count * (sums[:crop_rows] / own_total) - dot(pairs, sums[crop_rows:], ((1,), (0,)))
    )
    feature_grad = (
        feature_unit - s_unit * jnp.sum(s_unit * feature_unit, axis=1, keepdims=True)
    ) / s_norm
    grad_unit = coef * (
        dot(all_s * (all_count / total), expo, ((0,), (0,)))
        - dot(all_mixed, assign, ((0,), (0,)))
    )
    along = jnp.sum(student_unit * grad_unit, axis=0, keepdims=True)
    proto_grad = (grad_unit - student_unit * along) / student_norm
    square = jnp.mean(proto_grad * proto_grad, axis=0, keepdims=True)
    direction = proto_grad / jnp.sqrt(square + square_eps)
    student_next = student_cols - rate * (direction + weight_decay * student_cols)
    student_next = lax.all_to_all(
        student_next, "dp", split_axis=0, concat_axis=1, tiled=True
    )
    teacher_next = momentum * teacher_proto + (1.0 - momentum) * student_next
    return (student_next, teacher_next, feature_grad)


def solution(mesh):
    in_specs = (
        P("dp", None),
        P("dp", None),
        P("dp", "proto"),
        P("dp", "proto"),
        P("dp", None),
        P(),
    )
    out_specs = (P("dp", "proto"), P("dp", "proto"), P("dp", None))
    return jax.shard_map(body, mesh=mesh, in_specs=in_specs, out_specs=out_specs, check_vma=False)
```

```python
import functools

import jax
import jax.numpy as jnp
from jax import lax
from jax.experimental import pallas as pl
from jax.experimental.pallas import tpu as pltpu
from jax.sharding import PartitionSpec as P

CROPS = 10
GLOBAL_CROPS = 2
ITERS = 3
WARM_STEPS = 12500
TOTAL_STEPS = 625000


student_temp = 0.1
loss_scale = 16777216.0
norm_eps = 1e-06
square_eps = 1e-06
rate_peak = 0.05
weight_decay = 0.04
momentum_base = 0.994
highest = lax.Precision.HIGHEST


def plan(step):
    value = step[0].astype(jnp.float32)
    ramp = jnp.minimum(1.0, value / WARM_STEPS)
    rate = rate_peak * (0.25 + 0.75 * ramp)
    teacher_temp = 0.04 + 0.03 * ramp
    momentum = 1.0 - (1.0 - momentum_base) * (jnp.cos(jnp.pi * value / TOTAL_STEPS) + 1.0) * 0.5
    return (rate, teacher_temp, momentum)


NN = (((1,), (0,)), ((), ()))
NT = (((1,), (1,)), ((), ()))
MESH = pl.DeviceIdType.MESH
LANES = 128
SUBLANES = 8
f32 = jnp.float32
bf16 = jnp.bfloat16


def dot(left, right, dims):
    return lax.dot_general(left, right, dims, precision=highest, preferred_element_type=f32)


def split(values):
    high = values.astype(bf16)
    return high, (values - high.astype(f32)).astype(bf16)


def dot3(left, right, dims):
    def one(a, b):
        return lax.dot_general(a, b, dims, preferred_element_type=f32)

    return one(left[0], right[0]) + (one(left[0], right[1]) + one(left[1], right[0]))


def fold(values):
    rows, columns = values.shape
    return jnp.sum(values.reshape(rows // SUBLANES, SUBLANES, columns), axis=0)


def kernel(
    parts, groups, coef,
    plan_ref, sf_ref, tf_ref, sp_ref, tp_ref, crops_ref, crops_t_ref,
    snext_ref, tnext_ref, fgrad_ref,
    sp_in, tp_in, s_in, t_in, own_s, own_t, unit_hi, unit_lo, expo_hi, expo_lo,
    lane_part, inv_total, weighted, assign, row_dp, row_pr, tot_dp, tot_pr,
    f_send, f_dp, f_part, f_pr, f_sum, g_send, g_dp, g_part, g_pr, moved, landed,
    dp_send, dp_recv, f_ssem, f_rsem, pr_send, pr_recv, back_send, back_recv, local_sem,
):
    me, mine = lax.axis_index("dp"), lax.axis_index("proto")
    crop_rows, width = sf_ref.shape
    teach_rows = tf_ref.shape[0]
    own_rows, columns = sp_ref.shape
    share = columns // parts
    rate, temp, momentum = plan_ref[0], plan_ref[1], plan_ref[2]
    dp_peers = [lax.rem(me + hop, parts) for hop in range(1, parts)]
    pr_peers = [lax.rem(mine + hop, groups) for hop in range(1, groups)]
    barrier = pltpu.get_barrier_semaphore()
    for peer in dp_peers:
        pl.semaphore_signal(barrier, inc=1, device_id={"dp": peer}, device_id_type=MESH)
    for peer in pr_peers:
        pl.semaphore_signal(barrier, inc=1, device_id={"proto": peer}, device_id_type=MESH)

    t_values = tf_ref[...]
    own_t[...] = t_values / jnp.sqrt(jnp.sum(t_values * t_values, axis=1, keepdims=True) + norm_eps)
    s_values = sf_ref[...]
    s_norm = jnp.sqrt(jnp.sum(s_values * s_values, axis=1, keepdims=True) + norm_eps)
    s_unit = s_values / s_norm
    teach = lax.broadcasted_iota(jnp.int32, (teach_rows, crop_rows), 0)
    same = crops_t_ref[0:1, :] == teach // GLOBAL_CROPS
    other = crops_t_ref[1:2, :] != teach % GLOBAL_CROPS
    pairs_t = jnp.where(same & other, 1.0, 0.0).astype(f32)
    mixed_at, count_at = crop_rows, crop_rows + teach_rows
    own_s[0:crop_rows, :] = s_unit
    own_s[mixed_at:count_at, :] = dot(pairs_t, s_unit, NN)
    own_s[count_at:, :] = jnp.zeros((SUBLANES, width), f32)
    own_s[count_at:, 0:crop_rows] = jnp.broadcast_to(
        jnp.sum(pairs_t, axis=0, keepdims=True), (SUBLANES, crop_rows)
    )
    pl.semaphore_wait(barrier, parts - 1 + groups - 1)

    def remote(kind, hop, axis, peer, src, dst, ssem, rsem):
        return pltpu.make_async_remote_copy(
            src_ref=src, dst_ref=dst, send_sem=ssem.at[kind, hop], recv_sem=rsem.at[kind, hop],
            device_id={axis: peer}, device_id_type=MESH,
        )

    def cols(which):
        return pl.ds(pl.multiple_of(which * share, share), share)

    def rows(which, size):
        return pl.ds(pl.multiple_of(which * size, size), size)

    own_block = rows(me, own_rows)
    teacher_moves, student_moves, sends = [], [], []
    for hop, peer in enumerate(dp_peers):
        teacher_moves.append(remote(0, hop, "dp", peer, tp_ref.at[:, cols(peer)], tp_in.at[own_block, :], dp_send, dp_recv))
        teacher_moves.append(remote(1, hop, "dp", peer, own_t, t_in.at[rows(me, teach_rows), :], dp_send, dp_recv))
        student_moves.append(remote(2, hop, "dp", peer, sp_ref.at[:, cols(peer)], sp_in.at[own_block, :], dp_send, dp_recv))
        student_moves.append(remote(3, hop, "dp", peer, own_s, s_in.at[me], dp_send, dp_recv))
    for move in teacher_moves + student_moves:
        move.start()
        sends.append(move)
    local_moves = [
        pltpu.make_async_copy(tp_ref.at[:, cols(me)], tp_in.at[own_block, :], local_sem.at[0]),
        pltpu.make_async_copy(sp_ref.at[:, cols(me)], sp_in.at[own_block, :], local_sem.at[1]),
    ]
    for move in local_moves:
        move.start()
    t_in[rows(me, teach_rows), :] = own_t[...]
    s_in[me] = own_s[...]
    for move in local_moves:
        move.wait()

    def exchange(values, first, second, kind):
        first[me] = values
        moves = [
            remote(kind, hop, "dp", peer, first.at[me], first.at[me], dp_send, dp_recv)
            for hop, peer in enumerate(dp_peers)
        ]
        return spread(moves, first, second, kind)

    def spread(moves, first, second, kind):
        for move in moves:
            move.start()
            sends.append(move)

        def finish():
            for move in moves:
                move.wait_recv()
            second[mine] = jnp.sum(first[...], axis=0)
            later = [
                remote(kind, hop, "proto", peer, second.at[mine], second.at[mine], pr_send, pr_recv)
                for hop, peer in enumerate(pr_peers)
            ]
            for move in later:
                move.start()
                sends.append(move)

            def last():
                for move in later:
                    move.wait_recv()
                return jnp.sum(second[...], axis=0)

            return last

        return finish

    for move in teacher_moves:
        move.wait_recv()
    teacher_cols = tp_in[...]
    teacher_norm = jnp.sqrt(jnp.sum(teacher_cols * teacher_cols, axis=0, keepdims=True) + norm_eps)
    assign[...] = jnp.exp(dot((teacher_cols / teacher_norm).T, t_in[...], NT) / temp)
    for turn in range(ITERS):
        values = assign[...]
        values = values / jnp.sum(values, axis=1, keepdims=True)
        total = exchange(fold(values), row_dp.at[turn], row_pr.at[turn], 4 + turn)()()
        assign[...] = values / jnp.sum(total, axis=0, keepdims=True)

    for move in student_moves:
        move.wait_recv()
    student_cols = sp_in[...]
    student_norm = jnp.sqrt(jnp.sum(student_cols * student_cols, axis=0, keepdims=True) + norm_eps)
    high, low = split(student_cols / student_norm)
    unit_hi[...] = high
    unit_lo[...] = low

    def f_move(step, block):
        return remote(0, step, "dp", block, f_send.at[block], f_dp.at[me], f_ssem, f_rsem)

    def crop_block(step, carry):
        block = lax.rem(me + 1 + step, parts)
        at = rows(block, crop_rows)
        unit = (unit_hi[...], unit_lo[...])
        expo = jnp.exp(dot3(split(s_in[block, 0:crop_rows, :]), unit, NN) / student_temp)
        part = expo[:, 0:LANES]
        for lane in range(1, share // LANES):
            part = part + expo[:, lane * LANES:(lane + 1) * LANES]
        lane_part[at, :] = part
        pieces = split(expo)
        expo_hi[at, :] = pieces[0]
        expo_lo[at, :] = pieces[1]
        f_send[block] = dot3(pieces, unit, NT)

        @pl.when(step < parts - 1)
        def _():
            f_move(step, block).start()

        return carry

    lax.fori_loop(0, parts, crop_block, 0)
    finish = exchange(fold(lane_part[...].T), tot_dp, tot_pr, 4 + ITERS)

    g_send[...] = dot3((unit_hi[...], unit_lo[...]), split(assign[...]), NN).T
    g_moves = [
        remote(5 + ITERS, hop, "dp", peer, g_send.at[rows(peer, teach_rows), :], g_dp.at[me], dp_send, dp_recv)
        for hop, peer in enumerate(dp_peers)
    ]
    for move in g_moves:
        move.start()
        sends.append(move)
    g_dp[me] = g_send[rows(me, teach_rows), :]
    last = finish()
    f_dp[me] = f_send[me]
    mixed = s_in[:, mixed_at:count_at, :].reshape(parts * teach_rows, width)
    mixed_t = split(mixed.T)
    total = jnp.sum(last(), axis=0, keepdims=True)
    inv_total[...] = jnp.broadcast_to(1.0 / total, (LANES, parts * crop_rows)).T
    for block in range(parts):
        at = slice(block * crop_rows, (block + 1) * crop_rows)
        count = jnp.broadcast_to(s_in[block, count_at:count_at + 1, :], (LANES, width)).T
        weight = count[0:crop_rows, :] * inv_total[at, :]
        weighted[at, :] = s_in[block, 0:crop_rows, :] * jnp.concatenate([weight] * (width // LANES), axis=1)
    weighted_t = split(weighted[...].T)

    chunk = share // 2
    back_moves = []
    for piece in range(2):
        at = slice(piece * chunk, (piece + 1) * chunk)
        grad = coef * (
            dot3(weighted_t, (expo_hi[:, at], expo_lo[:, at]), NN)
            - dot3(mixed_t, split(assign[at, :]), NT)
        )
        now = sp_in[:, at]
        norm = jnp.sqrt(jnp.sum(now * now, axis=0, keepdims=True) + norm_eps)
        unit = now / norm
        proto_grad = (grad - unit * jnp.sum(unit * grad, axis=0, keepdims=True)) / norm
        square = jnp.sum(proto_grad * proto_grad, axis=0, keepdims=True) / width
        direction = proto_grad / jnp.sqrt(square + square_eps)
        moved[:, at] = now - rate * (direction + weight_decay * now)
        place = pl.ds(pl.multiple_of(me * share + piece * chunk, chunk), chunk)
        for hop, peer in enumerate(dp_peers):
            move = remote(piece, hop, "dp", peer, moved.at[rows(peer, own_rows), at], landed.at[:, place], back_send, back_recv)
            move.start()
            back_moves.append(move)
        landed[:, place] = moved[own_block, at]

    f_moves = [f_move(step, peer) for step, peer in enumerate(dp_peers)]
    for move in f_moves:
        move.wait_recv()
    f_part[...] = jnp.sum(f_dp[...], axis=0)
    for move in g_moves:
        move.wait_recv()
    g_pr[mine] = jnp.sum(g_dp[...], axis=0)
    f_pr[mine] = f_part[...]
    z_moves = []
    for hop, peer in enumerate(pr_peers):
        z_moves.append(remote(5 + ITERS, hop, "proto", peer, f_pr.at[mine], f_pr.at[mine], pr_send, pr_recv))
        z_moves.append(remote(6 + ITERS, hop, "proto", peer, g_pr.at[mine], g_pr.at[mine], pr_send, pr_recv))
    for move in z_moves:
        move.start()
        sends.append(move)
    for move in z_moves:
        move.wait_recv()
    teach = lax.broadcasted_iota(jnp.int32, (crop_rows, teach_rows), 1)
    same = crops_ref[:, 0:1] == teach // GLOBAL_CROPS
    other = crops_ref[:, 1:2] != teach % GLOBAL_CROPS
    pairs = jnp.where(same & other, 1.0, 0.0).astype(f32)
    count = jnp.sum(pairs, axis=1, keepdims=True)
    inverse = jnp.concatenate([inv_total[rows(me, crop_rows), :]] * (width // LANES), axis=1)
    feature_unit = coef * (
        count * (jnp.sum(f_pr[...], axis=0) * inverse) - dot(pairs, jnp.sum(g_pr[...], axis=0), NN)
    )
    s_values = sf_ref[...]
    s_norm = jnp.sqrt(jnp.sum(s_values * s_values, axis=1, keepdims=True) + norm_eps)
    s_unit = s_values / s_norm
    fgrad_ref[...] = (
        feature_unit - s_unit * jnp.sum(s_unit * feature_unit, axis=1, keepdims=True)
    ) / s_norm

    for move in back_moves:
        move.wait_recv()
    student_next = landed[...]
    snext_ref[...] = student_next
    tnext_ref[...] = momentum * tp_ref[...] + (1.0 - momentum) * student_next
    for move in sends + f_moves + back_moves:
        move.wait_send()


def body(student_feats, teacher_feats, student_proto, teacher_proto, crops, step):
    parts, groups = lax.axis_size("dp"), lax.axis_size("proto")
    crop_rows, width = student_feats.shape
    teach_rows = teacher_feats.shape[0]
    own_rows, columns = student_proto.shape
    share = columns // parts
    images = teach_rows // GLOBAL_CROPS * parts
    pair_total = GLOBAL_CROPS * (GLOBAL_CROPS - 1) + (CROPS - GLOBAL_CROPS) * GLOBAL_CROPS
    coef = loss_scale / (pair_total * images * student_temp)
    all_s, all_t = parts * crop_rows, parts * teach_rows
    packed = crop_rows + teach_rows + SUBLANES
    kinds = 7 + ITERS

    def vmem(*shape, dtype=f32):
        return pltpu.VMEM(shape, dtype)

    def sems(*shape):
        return pltpu.SemaphoreType.DMA(shape)

    whole = pl.BlockSpec(memory_space=pltpu.VMEM)
    shapes = [student_proto, teacher_proto, student_feats]
    return pl.pallas_call(
        functools.partial(kernel, parts, groups, coef),
        out_shape=[jax.ShapeDtypeStruct(one.shape, f32) for one in shapes],
        in_specs=[pl.BlockSpec(memory_space=pltpu.SMEM)] + [whole] * 6,
        out_specs=[whole] * 3,
        scratch_shapes=[
            vmem(width, share), vmem(width, share),
            vmem(parts, packed, width), vmem(all_t, width),
            vmem(packed, width), vmem(teach_rows, width),
            vmem(width, share, dtype=bf16), vmem(width, share, dtype=bf16),
            vmem(all_s, share, dtype=bf16), vmem(all_s, share, dtype=bf16),
            vmem(all_s, LANES), vmem(all_s, LANES), vmem(all_s, width),
            vmem(share, all_t),
            vmem(ITERS, parts, SUBLANES, all_t), vmem(ITERS, groups, SUBLANES, all_t),
            vmem(parts, SUBLANES, all_s), vmem(groups, SUBLANES, all_s),
            vmem(parts, crop_rows, width), vmem(parts, crop_rows, width),
            vmem(crop_rows, width), vmem(groups, crop_rows, width), vmem(crop_rows, width),
            vmem(all_t, width), vmem(parts, teach_rows, width),
            vmem(teach_rows, width), vmem(groups, teach_rows, width),
            vmem(width, share), vmem(own_rows, columns),
            sems(kinds, parts), sems(kinds, parts), sems(1, parts), sems(1, parts),
            sems(kinds, groups), sems(kinds, groups), sems(2, parts), sems(2, parts), sems(2),
        ],
        compiler_params=pltpu.CompilerParams(
            collective_id=0, has_side_effects=True, vmem_limit_bytes=56 * 1024 * 1024
        ),
    )(jnp.stack(plan(step)), student_feats, teacher_feats, student_proto, teacher_proto, crops, crops.T)


def solution(mesh):
    in_specs = (
        P("dp", None),
        P("dp", None),
        P("dp", "proto"),
        P("dp", "proto"),
        P("dp", None),
        P(),
    )
    out_specs = (P("dp", "proto"), P("dp", "proto"), P("dp", None))
    return jax.shard_map(body, mesh=mesh, in_specs=in_specs, out_specs=out_specs, check_vma=False)
```

```python
import functools

import jax
import jax.numpy as jnp
from jax import lax
from jax.experimental import pallas as pl
from jax.experimental.pallas import tpu as pltpu
from jax.sharding import PartitionSpec as P

CROPS = 10
GLOBAL_CROPS = 2
ITERS = 3
WARM_STEPS = 12500
TOTAL_STEPS = 625000


student_temp = 0.1
loss_scale = 16777216.0
norm_eps = 1e-06
square_eps = 1e-06
rate_peak = 0.05
weight_decay = 0.04
momentum_base = 0.994
highest = lax.Precision.HIGHEST


def plan(step):
    value = step[0].astype(jnp.float32)
    ramp = jnp.minimum(1.0, value / WARM_STEPS)
    rate = rate_peak * (0.25 + 0.75 * ramp)
    teacher_temp = 0.04 + 0.03 * ramp
    momentum = 1.0 - (1.0 - momentum_base) * (jnp.cos(jnp.pi * value / TOTAL_STEPS) + 1.0) * 0.5
    return (rate, teacher_temp, momentum)


NN = (((1,), (0,)), ((), ()))
NT = (((1,), (1,)), ((), ()))
MESH = pl.DeviceIdType.MESH
LANES = 128
SUBLANES = 8
f32 = jnp.float32
bf16 = jnp.bfloat16


def dot(left, right, dims):
    return lax.dot_general(left, right, dims, precision=highest, preferred_element_type=f32)


def split(values):
    high = values.astype(bf16)
    return high, (values - high.astype(f32)).astype(bf16)


def dot3(left, right, dims):
    def one(a, b):
        return lax.dot_general(a, b, dims, preferred_element_type=f32)

    return one(left[0], right[0]) + (one(left[0], right[1]) + one(left[1], right[0]))


def fold(values):
    rows, columns = values.shape
    return jnp.sum(values.reshape(rows // SUBLANES, SUBLANES, columns), axis=0)


def kernel(
    parts, groups, coef,
    plan_ref, sf_ref, tf_ref, sp_ref, tp_ref, crops_ref, crops_t_ref,
    step_ref, fgrad_ref,
    sp_in, tp_in, s_in, t_in, own_s, own_t, unit_hi, unit_lo, expo_hi, expo_lo,
    lane_part, inv_total, weighted, assign, row_dp, row_pr, tot_dp, tot_pr,
    f_send, f_pair, f_dp, f_part, f_pr, f_sum, g_send, g_dp, g_pr, moved,
    dp_send, dp_recv, pr_send, pr_recv, local_sem,
):
    me, mine = lax.axis_index("dp"), lax.axis_index("proto")
    crop_rows, width = sf_ref.shape
    teach_rows = tf_ref.shape[0]
    own_rows, columns = sp_ref.shape
    share = columns // parts
    half = parts // 2
    temp = plan_ref[1]
    parity = lax.rem(me, 2)
    partner = me + 1 - 2 * parity
    twins = [lax.rem(me + 2 * hop, parts) for hop in range(1, half)]
    senders = [lax.rem(me + parts - 2 * hop, parts) for hop in range(1, half)]
    dp_peers = [lax.rem(me + hop, parts) for hop in range(1, parts)]
    pr_peers = [lax.rem(mine + hop, groups) for hop in range(1, groups)]
    barrier = pltpu.get_barrier_semaphore()
    for peer in dp_peers:
        pl.semaphore_signal(barrier, inc=1, device_id={"dp": peer}, device_id_type=MESH)
    for peer in pr_peers:
        pl.semaphore_signal(barrier, inc=1, device_id={"proto": peer}, device_id_type=MESH)
    sends = []

    def cols(which):
        return pl.ds(pl.multiple_of(which * share, share), share)

    def rows(which, size):
        return pl.ds(pl.multiple_of(which * size, size), size)

    def dp_move(kind, hop, peer, src, dst):
        return pltpu.make_async_remote_copy(
            src_ref=src, dst_ref=dst, send_sem=dp_send.at[kind, hop], recv_sem=dp_recv.at[kind, hop],
            device_id={"dp": peer}, device_id_type=MESH,
        )

    def pr_move(kind, hop, peer, src, dst):
        return pltpu.make_async_remote_copy(
            src_ref=src, dst_ref=dst, send_sem=pr_send.at[kind, hop], recv_sem=pr_recv.at[kind, hop],
            device_id={"proto": peer}, device_id_type=MESH,
        )

    def start(moves):
        for move in moves:
            move.start()
            sends.append(move)
        return moves

    def arrive(moves):
        for move in moves:
            move.wait_recv()

    own_block = rows(me, own_rows)
    local_moves = [
        pltpu.make_async_copy(tp_ref.at[:, cols(me)], tp_in.at[own_block, :], local_sem.at[0]),
        pltpu.make_async_copy(sp_ref.at[:, cols(me)], sp_in.at[own_block, :], local_sem.at[1]),
    ]
    for move in local_moves:
        move.start()
    t_values = tf_ref[...]
    own_t[...] = t_values / jnp.sqrt(jnp.sum(t_values * t_values, axis=1, keepdims=True) + norm_eps)
    pl.semaphore_wait(barrier, parts - 1 + groups - 1)

    teacher_moves = start(
        [dp_move(0, hop, peer, tp_ref.at[:, cols(peer)], tp_in.at[own_block, :]) for hop, peer in enumerate(dp_peers)]
        + [dp_move(1, hop, peer, own_t, t_in.at[rows(me, teach_rows), :]) for hop, peer in enumerate(dp_peers)]
    )
    t_in[rows(me, teach_rows), :] = own_t[...]

    s_values = sf_ref[...]
    s_norm = jnp.sqrt(jnp.sum(s_values * s_values, axis=1, keepdims=True) + norm_eps)
    s_unit = s_values / s_norm
    teach = lax.broadcasted_iota(jnp.int32, (teach_rows, crop_rows), 0)
    same = crops_t_ref[0:1, :] == teach // GLOBAL_CROPS
    other = crops_t_ref[1:2, :] != teach % GLOBAL_CROPS
    pairs_t = jnp.where(same & other, 1.0, 0.0).astype(f32)
    mixed_at, count_at = crop_rows, crop_rows + teach_rows
    own_s[0:crop_rows, :] = s_unit
    own_s[mixed_at:count_at, :] = dot(pairs_t, s_unit, NN)
    own_s[count_at:, :] = jnp.zeros((SUBLANES, width), f32)
    own_s[count_at:, 0:crop_rows] = jnp.broadcast_to(
        jnp.sum(pairs_t, axis=0, keepdims=True), (SUBLANES, crop_rows)
    )
    near_move = start([dp_move(3, 0, partner, own_s, s_in.at[me])])
    twin_moves = start([dp_move(3, hop + 1, peer, own_s, s_in.at[me]) for hop, peer in enumerate(twins)])
    proto_moves = start(
        [dp_move(2, hop, peer, sp_ref.at[:, cols(peer)], sp_in.at[own_block, :]) for hop, peer in enumerate(dp_peers)]
    )
    s_in[me] = own_s[...]
    for move in local_moves:
        move.wait()

    def first_hop(values, first, kind):
        first[me] = values
        return start(
            [dp_move(kind, hop, peer, first.at[me], first.at[me]) for hop, peer in enumerate(dp_peers)]
        )

    def second_hop(moves, first, second, kind):
        arrive(moves)
        second[mine] = jnp.sum(first[...], axis=0)
        return start(
            [pr_move(kind, hop, peer, second.at[mine], second.at[mine]) for hop, peer in enumerate(pr_peers)]
        )

    def result(moves, second):
        arrive(moves)
        return jnp.sum(jnp.sum(second[...], axis=0), axis=0, keepdims=True)

    def balance(scale):
        values = assign[...]
        if scale is not None:
            values = values * scale
        values = values * (1.0 / jnp.sum(values, axis=1, keepdims=True))
        assign[...] = values
        return fold(values)

    def f_move(step, block):
        return dp_move(9, step, partner, f_send.at[block], f_pair.at[block // 2])

    def crop_blocks(base, near):
        def crop_block(step, carry):
            block = lax.rem(base + 2 * step, parts)
            at = rows(block, crop_rows)
            unit = (unit_hi[...], unit_lo[...])
            expo = jnp.exp(dot3(split(s_in[block, 0:crop_rows, :]), unit, NN) / student_temp)
            part = expo[:, 0:LANES]
            for lane in range(1, share // LANES):
                part = part + expo[:, lane * LANES:(lane + 1) * LANES]
            lane_part[at, :] = part
            pieces = split(expo)
            expo_hi[at, :] = pieces[0]
            expo_lo[at, :] = pieces[1]
            f_send[block] = dot3(pieces, unit, NT)
            if near:
                f_move(step, block).start()
            return carry

        lax.fori_loop(0, half, crop_block, 0)

    arrive(teacher_moves)
    teacher_cols = tp_in[...]
    teacher_norm = jnp.sqrt(jnp.sum(teacher_cols * teacher_cols, axis=0, keepdims=True) + norm_eps)
    assign[...] = jnp.exp(dot((teacher_cols / teacher_norm).T, t_in[...], NT) / temp)
    near = first_hop(balance(None), row_dp.at[0], 4)
    near = second_hop(near, row_dp.at[0], row_pr.at[0], 0)
    arrive(twin_moves)
    onward = start(
        [dp_move(8, hop, partner, s_in.at[block], s_in.at[block]) for hop, block in enumerate(senders)]
    )
    scale = 1.0 / result(near, row_pr.at[0])
    near = first_hop(balance(scale), row_dp.at[1], 5)

    arrive(proto_moves)
    student_cols = sp_in[...]
    student_norm = jnp.sqrt(jnp.sum(student_cols * student_cols, axis=0, keepdims=True) + norm_eps)
    high, low = split(student_cols / student_norm)
    unit_hi[...] = high
    unit_lo[...] = low
    arrive(near_move + onward)
    crop_blocks(partner, True)
    near = second_hop(near, row_dp.at[1], row_pr.at[1], 1)
    crop_blocks(me, False)
    tot_near = first_hop(fold(lane_part[...].T), tot_dp, 7)
    scale = 1.0 / result(near, row_pr.at[1])
    near = first_hop(balance(scale), row_dp.at[2], 6)

    f_near = [f_move(step, lax.rem(partner + 2 * step, parts)) for step in range(half)]
    arrive(f_near)
    sends.extend(f_near)
    slot = me // 2
    f_moves = []
    for hop, peer in enumerate(twins):
        f_send[peer] = f_send[peer] + f_pair[peer // 2]
        f_moves.append(dp_move(10, hop, peer, f_send.at[peer], f_dp.at[slot]))
        start(f_moves[-1:])
    f_dp[slot] = f_send[me] + f_pair[slot]
    tot_near = second_hop(tot_near, tot_dp, tot_pr, 3)
    near = second_hop(near, row_dp.at[2], row_pr.at[2], 2)
    mixed = s_in[:, mixed_at:count_at, :].reshape(parts * teach_rows, width).T
    targets = dot3((unit_hi[...], unit_lo[...]), split(assign[...]), NN)
    total = result(tot_near, tot_pr)
    inv_total[...] = jnp.broadcast_to(1.0 / total, (LANES, parts * crop_rows)).T
    for block in range(parts):
        at = slice(block * crop_rows, (block + 1) * crop_rows)
        count = jnp.broadcast_to(s_in[block, count_at:count_at + 1, :], (LANES, width)).T
        weight = count[0:crop_rows, :] * inv_total[at, :]
        weighted[at, :] = s_in[block, 0:crop_rows, :] * jnp.concatenate([weight] * (width // LANES), axis=1)
    weighted_t = split(weighted[...].T)
    scale = 1.0 / result(near, row_pr.at[2])
    mixed_t = split(mixed * scale)
    g_send[...] = (targets * scale).T

    chunk = share // 2
    back_moves = []
    for piece in range(2):
        at = slice(piece * chunk, (piece + 1) * chunk)
        grad = coef * (
            dot3(weighted_t, (expo_hi[:, at], expo_lo[:, at]), NN)
            - dot3(mixed_t, split(assign[at, :]), NT)
        )
        now = sp_in[:, at]
        norm = jnp.sqrt(jnp.sum(now * now, axis=0, keepdims=True) + norm_eps)
        unit = now / norm
        proto_grad = (grad - unit * jnp.sum(unit * grad, axis=0, keepdims=True)) / norm
        square = jnp.sum(proto_grad * proto_grad, axis=0, keepdims=True) / width
        moved[:, at] = proto_grad / jnp.sqrt(square + square_eps)
        place = pl.ds(pl.multiple_of(me * share + piece * chunk, chunk), chunk)
        back_moves += start([
            dp_move(12 + piece, hop, peer, moved.at[rows(peer, own_rows), at], step_ref.at[:, place])
            for hop, peer in enumerate(dp_peers)
        ])
        step_ref[:, place] = moved[own_block, at]
        if piece == 0:
            g_moves = start([
                dp_move(11, hop, peer, g_send.at[rows(peer, teach_rows), :], g_dp.at[me])
                for hop, peer in enumerate(dp_peers)
            ])
            g_dp[me] = g_send[rows(me, teach_rows), :]

    piece_rows = f_part.shape[0] // groups
    arrive(f_moves)
    f_part[0:crop_rows, :] = jnp.sum(f_dp[...], axis=0)
    if f_part.shape[0] > crop_rows:
        f_part[crop_rows:, :] = jnp.zeros((f_part.shape[0] - crop_rows, width), f32)
    f_across = start(
        [pr_move(4, hop, peer, f_part.at[rows(peer, piece_rows), :], f_pr.at[mine]) for hop, peer in enumerate(pr_peers)]
    )
    f_pr[mine] = f_part[rows(mine, piece_rows), :]
    arrive(g_moves)
    g_pr[mine] = jnp.sum(g_dp[...], axis=0)
    g_across = start(
        [pr_move(5, hop, peer, g_pr.at[mine], g_pr.at[mine]) for hop, peer in enumerate(pr_peers)]
    )
    arrive(f_across)
    own_piece = rows(mine, piece_rows)
    f_sum[own_piece, :] = jnp.sum(f_pr[...], axis=0)
    f_last = start(
        [pr_move(6, hop, peer, f_sum.at[own_piece, :], f_sum.at[own_piece, :]) for hop, peer in enumerate(pr_peers)]
    )
    teach = lax.broadcasted_iota(jnp.int32, (crop_rows, teach_rows), 1)
    same = crops_ref[:, 0:1] == teach // GLOBAL_CROPS
    other = crops_ref[:, 1:2] != teach % GLOBAL_CROPS
    pairs = jnp.where(same & other, 1.0, 0.0).astype(f32)
    count = jnp.sum(pairs, axis=1, keepdims=True)
    inverse = jnp.concatenate([inv_total[rows(me, crop_rows), :]] * (width // LANES), axis=1)
    s_values = sf_ref[...]
    s_norm = jnp.sqrt(jnp.sum(s_values * s_values, axis=1, keepdims=True) + norm_eps)
    s_unit = s_values / s_norm
    arrive(g_across)
    wanted = dot(pairs, jnp.sum(g_pr[...], axis=0), NN)
    arrive(f_last)
    feature_unit = coef * (count * (f_sum[0:crop_rows, :] * inverse) - wanted)
    fgrad_ref[...] = (
        feature_unit - s_unit * jnp.sum(s_unit * feature_unit, axis=1, keepdims=True)
    ) / s_norm
    arrive(back_moves)
    for move in sends:
        move.wait_send()


def body(student_feats, teacher_feats, student_proto, teacher_proto, crops, step):
    parts, groups = lax.axis_size("dp"), lax.axis_size("proto")
    crop_rows, width = student_feats.shape
    teach_rows = teacher_feats.shape[0]
    own_rows, columns = student_proto.shape
    share = columns // parts
    images = teach_rows // GLOBAL_CROPS * parts
    pair_total = GLOBAL_CROPS * (GLOBAL_CROPS - 1) + (CROPS - GLOBAL_CROPS) * GLOBAL_CROPS
    coef = loss_scale / (pair_total * images * student_temp)
    all_s, all_t = parts * crop_rows, parts * teach_rows
    packed = crop_rows + teach_rows + SUBLANES
    kinds = 14
    piece_rows = -(-crop_rows // (groups * SUBLANES)) * SUBLANES
    rate, teacher_temp, momentum = plan(step)

    def vmem(*shape, dtype=f32):
        return pltpu.VMEM(shape, dtype)

    def sems(*shape):
        return pltpu.SemaphoreType.DMA(shape)

    whole = pl.BlockSpec(memory_space=pltpu.VMEM)
    shapes = [student_proto, student_feats]
    direction, feature_grad = pl.pallas_call(
        functools.partial(kernel, parts, groups, coef),
        out_shape=[jax.ShapeDtypeStruct(one.shape, f32) for one in shapes],
        in_specs=[pl.BlockSpec(memory_space=pltpu.SMEM)] + [whole] * 6,
        out_specs=[whole] * 2,
        scratch_shapes=[
            vmem(width, share), vmem(width, share),
            vmem(parts, packed, width), vmem(all_t, width),
            vmem(packed, width), vmem(teach_rows, width),
            vmem(width, share, dtype=bf16), vmem(width, share, dtype=bf16),
            vmem(all_s, share, dtype=bf16), vmem(all_s, share, dtype=bf16),
            vmem(all_s, LANES), vmem(all_s, LANES), vmem(all_s, width),
            vmem(share, all_t),
            vmem(ITERS, parts, SUBLANES, all_t), vmem(ITERS, groups, SUBLANES, all_t),
            vmem(parts, SUBLANES, all_s), vmem(groups, SUBLANES, all_s),
            vmem(parts, crop_rows, width), vmem(parts // 2, crop_rows, width),
            vmem(parts // 2, crop_rows, width), vmem(groups * piece_rows, width),
            vmem(groups, piece_rows, width), vmem(groups * piece_rows, width),
            vmem(all_t, width), vmem(parts, teach_rows, width), vmem(groups, teach_rows, width),
            vmem(width, share),
            sems(kinds, parts), sems(kinds, parts), sems(7, groups), sems(7, groups), sems(2),
        ],
        compiler_params=pltpu.CompilerParams(
            collective_id=0, has_side_effects=True, vmem_limit_bytes=56 * 1024 * 1024
        ),
    )(jnp.stack([rate, teacher_temp]), student_feats, teacher_feats, student_proto, teacher_proto, crops, crops.T)
    student_next = student_proto - rate * (direction + weight_decay * student_proto)
    teacher_next = momentum * teacher_proto + (1.0 - momentum) * student_next
    return (student_next, teacher_next, feature_grad)


def solution(mesh):
    in_specs = (
        P("dp", None),
        P("dp", None),
        P("dp", "proto"),
        P("dp", "proto"),
        P("dp", None),
        P(),
    )
    out_specs = (P("dp", "proto"), P("dp", "proto"), P("dp", None))
    return jax.shard_map(body, mesh=mesh, in_specs=in_specs, out_specs=out_specs, check_vma=False)
```

```python
import functools

import jax
import jax.numpy as jnp
from jax import lax
from jax.experimental import pallas as pl
from jax.experimental.pallas import tpu as pltpu
from jax.sharding import PartitionSpec as P

CROPS = 10
GLOBAL_CROPS = 2
ITERS = 3
WARM_STEPS = 12500
TOTAL_STEPS = 625000


student_temp = 0.1
loss_scale = 16777216.0
norm_eps = 1e-06
square_eps = 1e-06
rate_peak = 0.05
weight_decay = 0.04
momentum_base = 0.994
highest = lax.Precision.HIGHEST


def plan(step):
    value = step[0].astype(jnp.float32)
    ramp = jnp.minimum(1.0, value / WARM_STEPS)
    rate = rate_peak * (0.25 + 0.75 * ramp)
    teacher_temp = 0.04 + 0.03 * ramp
    momentum = 1.0 - (1.0 - momentum_base) * (jnp.cos(jnp.pi * value / TOTAL_STEPS) + 1.0) * 0.5
    return (rate, teacher_temp, momentum)


NN = (((1,), (0,)), ((), ()))
NT = (((1,), (1,)), ((), ()))
MESH = pl.DeviceIdType.MESH
LANES = 128
SUBLANES = 8
CHUNKS = 4
f32 = jnp.float32
bf16 = jnp.bfloat16


def dot(left, right, dims):
    return lax.dot_general(left, right, dims, precision=highest, preferred_element_type=f32)


def split(values):
    high = values.astype(bf16)
    return high, (values - high.astype(f32)).astype(bf16)


def dot3(left, right, dims):
    def one(a, b):
        return lax.dot_general(a, b, dims, preferred_element_type=f32)

    return one(left[0], right[0]) + (one(left[0], right[1]) + one(left[1], right[0]))


def fold(values):
    rows, columns = values.shape
    return jnp.sum(values.reshape(rows // SUBLANES, SUBLANES, columns), axis=0)


def kernel(
    parts, groups, coef,
    plan_ref, sf_ref, tf_ref, sp_ref, tp_ref, crops_ref, crops_t_ref,
    step_ref, fgrad_ref,
    sp_in, tp_in, s_in, t_in, own_s, own_t, unit_hi, unit_lo, expo_hi, expo_lo,
    s_hi, s_lo, lane_part, counted, counted_t, mixed_t, assign, row_dp, row_pr, tot_dp, tot_pr,
    f_send, f_pair, f_dp, f_part, f_pr, f_sum, g_send, g_dp, g_pr, moved,
    dp_send, dp_recv, pr_send, pr_recv, local_sem,
):
    me, mine = lax.axis_index("dp"), lax.axis_index("proto")
    crop_rows, width = sf_ref.shape
    teach_rows = tf_ref.shape[0]
    own_rows, columns = sp_ref.shape
    share = columns // parts
    half = parts // 2
    temp = plan_ref[1]
    parity = lax.rem(me, 2)
    partner = me + 1 - 2 * parity
    twins = [lax.rem(me + 2 * hop, parts) for hop in range(1, half)]
    senders = [lax.rem(me + parts - 2 * hop, parts) for hop in range(1, half)]
    dp_peers = [lax.rem(me + hop, parts) for hop in range(1, parts)]
    pr_peers = [lax.rem(mine + hop, groups) for hop in range(1, groups)]
    barrier = pltpu.get_barrier_semaphore()
    for peer in dp_peers:
        pl.semaphore_signal(barrier, inc=1, device_id={"dp": peer}, device_id_type=MESH)
    for peer in pr_peers:
        pl.semaphore_signal(barrier, inc=1, device_id={"proto": peer}, device_id_type=MESH)
    sends = []

    def cols(which):
        return pl.ds(pl.multiple_of(which * share, share), share)

    def rows(which, size):
        return pl.ds(pl.multiple_of(which * size, size), size)

    def dp_move(kind, hop, peer, src, dst):
        return pltpu.make_async_remote_copy(
            src_ref=src, dst_ref=dst, send_sem=dp_send.at[kind, hop], recv_sem=dp_recv.at[kind, hop],
            device_id={"dp": peer}, device_id_type=MESH,
        )

    def pr_move(kind, hop, peer, src, dst):
        return pltpu.make_async_remote_copy(
            src_ref=src, dst_ref=dst, send_sem=pr_send.at[kind, hop], recv_sem=pr_recv.at[kind, hop],
            device_id={"proto": peer}, device_id_type=MESH,
        )

    def start(moves):
        for move in moves:
            move.start()
            sends.append(move)
        return moves

    def arrive(moves):
        for move in moves:
            move.wait_recv()

    own_block = rows(me, own_rows)
    local_moves = [
        pltpu.make_async_copy(tp_ref.at[:, cols(me)], tp_in.at[own_block, :], local_sem.at[0]),
        pltpu.make_async_copy(sp_ref.at[:, cols(me)], sp_in.at[own_block, :], local_sem.at[1]),
    ]
    for move in local_moves:
        move.start()
    t_values = tf_ref[...]
    own_t[...] = t_values / jnp.sqrt(jnp.sum(t_values * t_values, axis=1, keepdims=True) + norm_eps)
    pl.semaphore_wait(barrier, parts - 1 + groups - 1)

    teacher_moves = start(
        [dp_move(0, hop, peer, tp_ref.at[:, cols(peer)], tp_in.at[own_block, :]) for hop, peer in enumerate(dp_peers)]
        + [dp_move(1, hop, peer, own_t, t_in.at[rows(me, teach_rows), :]) for hop, peer in enumerate(dp_peers)]
    )
    t_in[rows(me, teach_rows), :] = own_t[...]

    s_values = sf_ref[...]
    s_norm = jnp.sqrt(jnp.sum(s_values * s_values, axis=1, keepdims=True) + norm_eps)
    s_unit = s_values / s_norm
    teach = lax.broadcasted_iota(jnp.int32, (teach_rows, crop_rows), 0)
    same = crops_t_ref[0:1, :] == teach // GLOBAL_CROPS
    other = crops_t_ref[1:2, :] != teach % GLOBAL_CROPS
    pairs_t = jnp.where(same & other, 1.0, 0.0).astype(f32)
    mixed_at, count_at = crop_rows, crop_rows + teach_rows
    own_s[0:crop_rows, :] = s_unit
    own_s[mixed_at:count_at, :] = dot(pairs_t, s_unit, NN)
    own_s[count_at:, :] = jnp.zeros((SUBLANES, width), f32)
    own_s[count_at:, 0:crop_rows] = jnp.broadcast_to(
        jnp.sum(pairs_t, axis=0, keepdims=True), (SUBLANES, crop_rows)
    )
    near_move = start([dp_move(3, 0, partner, own_s, s_in.at[me])])
    twin_moves = start([dp_move(3, hop + 1, peer, own_s, s_in.at[me]) for hop, peer in enumerate(twins)])
    proto_moves = start(
        [dp_move(2, hop, peer, sp_ref.at[:, cols(peer)], sp_in.at[own_block, :]) for hop, peer in enumerate(dp_peers)]
    )
    s_in[me] = own_s[...]
    for move in local_moves:
        move.wait()

    def first_hop(values, first, kind):
        first[me] = values
        return start(
            [dp_move(kind, hop, peer, first.at[me], first.at[me]) for hop, peer in enumerate(dp_peers)]
        )

    def second_hop(moves, first, second, kind):
        arrive(moves)
        second[mine] = jnp.sum(first[...], axis=0)
        return start(
            [pr_move(kind, hop, peer, second.at[mine], second.at[mine]) for hop, peer in enumerate(pr_peers)]
        )

    def result(moves, second):
        arrive(moves)
        return jnp.sum(jnp.sum(second[...], axis=0), axis=0, keepdims=True)

    def balance(scale):
        values = assign[...]
        if scale is not None:
            values = values * scale
        values = values * (1.0 / jnp.sum(values, axis=1, keepdims=True))
        assign[...] = values
        return fold(values)

    tile = 2 * crop_rows
    half_rows = half * crop_rows

    def place_of(block):
        return (block // 2) + half * lax.rem(block, 2)

    def score_tile(step, carry):
        at = rows(step, tile)
        unit = (unit_hi[...], unit_lo[...])
        expo = jnp.exp(dot3((s_hi[at, :], s_lo[at, :]), unit, NN) / student_temp)
        part = expo[:, 0:LANES]
        for lane in range(1, share // LANES):
            part = part + expo[:, lane * LANES:(lane + 1) * LANES]
        lane_part[at, :] = part
        pieces = split(expo)
        expo_hi[at, :] = pieces[0]
        expo_lo[at, :] = pieces[1]
        return carry

    def f_move(step):
        at = pl.ds(pl.multiple_of((1 - parity) * half_rows + step * tile, tile), tile)
        return dp_move(9, step, partner, f_send.at[at, :], f_pair.at[rows(step, tile), :])

    def feature_tiles(which, near):
        def feature_tile(step, carry):
            at = pl.ds(pl.multiple_of(which * half_rows + step * tile, tile), tile)
            f_send[at, :] = dot3((expo_hi[at, :], expo_lo[at, :]), (unit_hi[...], unit_lo[...]), NT)
            if near:
                f_move(step).start()
            return carry

        lax.fori_loop(0, half // 2, feature_tile, 0)

    arrive(teacher_moves)
    teacher_cols = tp_in[...]
    teacher_norm = jnp.sqrt(jnp.sum(teacher_cols * teacher_cols, axis=0, keepdims=True) + norm_eps)
    assign[...] = jnp.exp(dot((teacher_cols / teacher_norm).T, t_in[...], NT) / temp)
    near = first_hop(balance(None), row_dp.at[0], 4)
    near = second_hop(near, row_dp.at[0], row_pr.at[0], 0)
    scale = 1.0 / result(near, row_pr.at[0])
    near = first_hop(balance(scale), row_dp.at[1], 5)
    arrive(twin_moves)
    onward = start(
        [dp_move(8, hop, partner, s_in.at[block], s_in.at[block]) for hop, block in enumerate(senders)]
    )
    near = second_hop(near, row_dp.at[1], row_pr.at[1], 1)
    scale = 1.0 / result(near, row_pr.at[1])
    near = first_hop(balance(scale), row_dp.at[2], 6)

    arrive(near_move + onward)
    for block in range(parts):
        first = (block // 2 + half * (block % 2)) * crop_rows
        at = slice(first, first + crop_rows)
        crops_now = s_in[block, 0:crop_rows, :]
        high, low = split(crops_now)
        s_hi[at, :] = high
        s_lo[at, :] = low
        count = jnp.broadcast_to(s_in[block, count_at:count_at + 1, :], (LANES, width)).T
        counted[at, :] = crops_now * jnp.concatenate([count[0:crop_rows, :]] * (width // LANES), axis=1)
    counted_t[...] = counted[...].T
    mixed_t[...] = s_in[:, mixed_at:count_at, :].reshape(parts * teach_rows, width).T

    arrive(proto_moves)
    student_cols = sp_in[...]
    student_norm = jnp.sqrt(jnp.sum(student_cols * student_cols, axis=0, keepdims=True) + norm_eps)
    high, low = split(student_cols / student_norm)
    unit_hi[...] = high
    unit_lo[...] = low
    near = second_hop(near, row_dp.at[2], row_pr.at[2], 2)
    lax.fori_loop(0, half, score_tile, 0)
    tot_near = first_hop(fold(lane_part[...].T), tot_dp, 7)
    feature_tiles(1 - parity, True)
    tot_near = second_hop(tot_near, tot_dp, tot_pr, 3)
    feature_tiles(parity, False)
    targets = dot3((unit_hi[...], unit_lo[...]), split(assign[...]), NN)
    scale = 1.0 / result(near, row_pr.at[2])
    mixed_pieces = split(mixed_t[...] * scale)
    g_send[...] = (targets * scale).T
    f_near = [f_move(step) for step in range(half // 2)]
    arrive(f_near)
    sends.extend(f_near)
    own_half = pl.ds(pl.multiple_of(parity * half_rows, half_rows), half_rows)
    f_send[own_half, :] = f_send[own_half, :] + f_pair[...]
    slot = me // 2
    f_moves = start([
        dp_move(10, hop, peer, f_send.at[rows(place_of(peer), crop_rows), :], f_dp.at[slot])
        for hop, peer in enumerate(twins)
    ])
    f_dp[slot] = f_send[rows(place_of(me), crop_rows), :]
    inverse_row = 1.0 / result(tot_near, tot_pr)
    weighted_t = split(counted_t[...] * inverse_row)
    lane_part[...] = jnp.broadcast_to(inverse_row, (LANES, parts * crop_rows)).T

    chunk = share // CHUNKS
    piece_rows = f_part.shape[0] // groups
    back_moves, home_moves = [], []
    for piece in range(CHUNKS):
        at = slice(piece * chunk, (piece + 1) * chunk)
        grad = coef * (
            dot3(weighted_t, (expo_hi[:, at], expo_lo[:, at]), NN)
            - dot3(mixed_pieces, split(assign[at, :]), NT)
        )
        now = sp_in[:, at]
        norm = jnp.sqrt(jnp.sum(now * now, axis=0, keepdims=True) + norm_eps)
        unit = now / norm
        proto_grad = (grad - unit * jnp.sum(unit * grad, axis=0, keepdims=True)) / norm
        square = jnp.sum(proto_grad * proto_grad, axis=0, keepdims=True) / width
        moved[:, at] = proto_grad / jnp.sqrt(square + square_eps)
        place = pl.ds(pl.multiple_of(me * share + piece * chunk, chunk), chunk)
        back_moves += start([
            dp_move(12 + piece, hop, peer, moved.at[rows(peer, own_rows), at], step_ref.at[:, place])
            for hop, peer in enumerate(dp_peers)
        ])
        home_moves.append(pltpu.make_async_copy(moved.at[own_block, at], step_ref.at[:, place], local_sem.at[2 + piece]))
        home_moves[-1].start()
        if piece == 0:
            g_moves = start([
                dp_move(11, hop, peer, g_send.at[rows(peer, teach_rows), :], g_dp.at[me])
                for hop, peer in enumerate(dp_peers)
            ])
            g_dp[me] = g_send[rows(me, teach_rows), :]
        if piece == 1:
            arrive(f_moves)
            f_part[0:crop_rows, :] = jnp.sum(f_dp[...], axis=0)
            if f_part.shape[0] > crop_rows:
                f_part[crop_rows:, :] = jnp.zeros((f_part.shape[0] - crop_rows, width), f32)
            f_across = start([
                pr_move(4, hop, peer, f_part.at[rows(peer, piece_rows), :], f_pr.at[mine])
                for hop, peer in enumerate(pr_peers)
            ])
            f_pr[mine] = f_part[rows(mine, piece_rows), :]
    arrive(f_across)
    own_piece = rows(mine, piece_rows)
    f_sum[own_piece, :] = jnp.sum(f_pr[...], axis=0)
    f_last = start(
        [pr_move(6, hop, peer, f_sum.at[own_piece, :], f_sum.at[own_piece, :]) for hop, peer in enumerate(pr_peers)]
    )
    arrive(g_moves)
    g_pr[mine] = jnp.sum(g_dp[...], axis=0)
    g_across = start(
        [pr_move(5, hop, peer, g_pr.at[mine], g_pr.at[mine]) for hop, peer in enumerate(pr_peers)]
    )
    teach = lax.broadcasted_iota(jnp.int32, (crop_rows, teach_rows), 1)
    same = crops_ref[:, 0:1] == teach // GLOBAL_CROPS
    other = crops_ref[:, 1:2] != teach % GLOBAL_CROPS
    pairs = jnp.where(same & other, 1.0, 0.0).astype(f32)
    count = jnp.sum(pairs, axis=1, keepdims=True)
    inverse = jnp.concatenate([lane_part[rows(place_of(me), crop_rows), :]] * (width // LANES), axis=1)
    s_values = sf_ref[...]
    s_norm = jnp.sqrt(jnp.sum(s_values * s_values, axis=1, keepdims=True) + norm_eps)
    s_unit = s_values / s_norm
    arrive(g_across)
    wanted = dot(pairs, jnp.sum(g_pr[...], axis=0), NN)
    arrive(f_last)
    feature_unit = coef * (count * (f_sum[0:crop_rows, :] * inverse) - wanted)
    fgrad_ref[...] = (
        feature_unit - s_unit * jnp.sum(s_unit * feature_unit, axis=1, keepdims=True)
    ) / s_norm
    arrive(back_moves)
    for move in home_moves:
        move.wait()
    for move in sends:
        move.wait_send()


def body(student_feats, teacher_feats, student_proto, teacher_proto, crops, step):
    parts, groups = lax.axis_size("dp"), lax.axis_size("proto")
    crop_rows, width = student_feats.shape
    teach_rows = teacher_feats.shape[0]
    own_rows, columns = student_proto.shape
    share = columns // parts
    images = teach_rows // GLOBAL_CROPS * parts
    pair_total = GLOBAL_CROPS * (GLOBAL_CROPS - 1) + (CROPS - GLOBAL_CROPS) * GLOBAL_CROPS
    coef = loss_scale / (pair_total * images * student_temp)
    all_s, all_t = parts * crop_rows, parts * teach_rows
    packed = crop_rows + teach_rows + SUBLANES
    kinds = 12 + CHUNKS
    piece_rows = -(-crop_rows // (groups * SUBLANES)) * SUBLANES
    rate, teacher_temp, momentum = plan(step)

    def vmem(*shape, dtype=f32):
        return pltpu.VMEM(shape, dtype)

    def sems(*shape):
        return pltpu.SemaphoreType.DMA(shape)

    whole, outside = pl.BlockSpec(memory_space=pltpu.VMEM), pl.BlockSpec(memory_space=pl.ANY)
    shapes = [student_proto, student_feats]
    direction, feature_grad = pl.pallas_call(
        functools.partial(kernel, parts, groups, coef),
        out_shape=[jax.ShapeDtypeStruct(one.shape, f32) for one in shapes],
        in_specs=[pl.BlockSpec(memory_space=pltpu.SMEM), whole, whole, outside, outside, whole, whole],
        out_specs=[outside, whole],
        scratch_shapes=[
            vmem(width, share), vmem(width, share),
            vmem(parts, packed, width), vmem(all_t, width),
            vmem(packed, width), vmem(teach_rows, width),
            vmem(width, share, dtype=bf16), vmem(width, share, dtype=bf16),
            vmem(all_s, share, dtype=bf16), vmem(all_s, share, dtype=bf16),
            vmem(all_s, width, dtype=bf16), vmem(all_s, width, dtype=bf16),
            vmem(all_s, LANES), vmem(all_s, width), vmem(width, all_s), vmem(width, all_t),
            vmem(share, all_t),
            vmem(ITERS, parts, SUBLANES, all_t), vmem(ITERS, groups, SUBLANES, all_t),
            vmem(parts, SUBLANES, all_s), vmem(groups, SUBLANES, all_s),
            vmem(all_s, width), vmem(all_s // 2, width),
            vmem(parts // 2, crop_rows, width), vmem(groups * piece_rows, width),
            vmem(groups, piece_rows, width), vmem(groups * piece_rows, width),
            vmem(all_t, width), vmem(parts, teach_rows, width), vmem(groups, teach_rows, width),
            vmem(width, share),
            sems(kinds, parts), sems(kinds, parts), sems(7, groups), sems(7, groups), sems(2 + CHUNKS),
        ],
        compiler_params=pltpu.CompilerParams(
            collective_id=0, has_side_effects=True, vmem_limit_bytes=56 * 1024 * 1024
        ),
    )(jnp.stack([rate, teacher_temp]), student_feats, teacher_feats, student_proto, teacher_proto, crops, crops.T)
    student_next = student_proto - rate * (direction + weight_decay * student_proto)
    teacher_next = momentum * teacher_proto + (1.0 - momentum) * student_next
    return (student_next, teacher_next, feature_grad)


def solution(mesh):
    in_specs = (
        P("dp", None),
        P("dp", None),
        P("dp", "proto"),
        P("dp", "proto"),
        P("dp", None),
        P(),
    )
    out_specs = (P("dp", "proto"), P("dp", "proto"), P("dp", None))
    return jax.shard_map(body, mesh=mesh, in_specs=in_specs, out_specs=out_specs, check_vma=False)
```

```python
import functools

import jax
import jax.numpy as jnp
from jax import lax
from jax.experimental import pallas as pl
from jax.experimental.pallas import tpu as pltpu
from jax.sharding import PartitionSpec as P

CROPS = 10
GLOBAL_CROPS = 2
ITERS = 3
WARM_STEPS = 12500
TOTAL_STEPS = 625000


student_temp = 0.1
loss_scale = 16777216.0
norm_eps = 1e-06
square_eps = 1e-06
rate_peak = 0.05
weight_decay = 0.04
momentum_base = 0.994
highest = lax.Precision.HIGHEST


def plan(step):
    value = step[0].astype(jnp.float32)
    ramp = jnp.minimum(1.0, value / WARM_STEPS)
    rate = rate_peak * (0.25 + 0.75 * ramp)
    teacher_temp = 0.04 + 0.03 * ramp
    momentum = 1.0 - (1.0 - momentum_base) * (jnp.cos(jnp.pi * value / TOTAL_STEPS) + 1.0) * 0.5
    return (rate, teacher_temp, momentum)


NN = (((1,), (0,)), ((), ()))
NT = (((1,), (1,)), ((), ()))
MESH = pl.DeviceIdType.MESH
LANES = 128
SUBLANES = 8
CHUNKS = 4
f32 = jnp.float32
bf16 = jnp.bfloat16


def dot(left, right, dims):
    return lax.dot_general(left, right, dims, precision=highest, preferred_element_type=f32)


def split(values):
    high = values.astype(bf16)
    return high, (values - high.astype(f32)).astype(bf16)


def dot3(left, right, dims):
    def one(a, b):
        return lax.dot_general(a, b, dims, preferred_element_type=f32)

    return one(left[0], right[0]) + (one(left[0], right[1]) + one(left[1], right[0]))


def fold(values):
    rows, columns = values.shape
    return jnp.sum(values.reshape(rows // SUBLANES, SUBLANES, columns), axis=0)


def kernel(
    parts, groups, coef,
    plan_ref, sf_ref, tf_ref, sp_ref, tp_ref, crops_ref, crops_t_ref,
    step_ref, fgrad_ref,
    sp_in, tp_in, s_in, t_in, own_s, own_t, unit_hi, unit_lo, expo_hi, expo_lo,
    s_hi, s_lo, lane_part, counted, counted_t, mixed_t, assign, row_dp, row_pr, tot_dp, tot_pr,
    f_send, f_pair, f_dp, f_part, f_pr, f_sum, g_send, g_dp, g_pr, moved,
    dp_send, dp_recv, pr_send, pr_recv, local_sem,
):
    me, mine = lax.axis_index("dp"), lax.axis_index("proto")
    crop_rows, width = sf_ref.shape
    teach_rows = tf_ref.shape[0]
    own_rows, columns = sp_ref.shape
    share = columns // parts
    half = parts // 2
    temp = plan_ref[1]
    parity = lax.rem(me, 2)
    partner = me + 1 - 2 * parity
    twins = [lax.rem(me + 2 * hop, parts) for hop in range(1, half)]
    senders = [lax.rem(me + parts - 2 * hop, parts) for hop in range(1, half)]
    dp_peers = [lax.rem(me + hop, parts) for hop in range(1, parts)]
    pr_peers = [lax.rem(mine + hop, groups) for hop in range(1, groups)]
    barrier = pltpu.get_barrier_semaphore()
    for peer in dp_peers:
        pl.semaphore_signal(barrier, inc=1, device_id={"dp": peer}, device_id_type=MESH)
    for peer in pr_peers:
        pl.semaphore_signal(barrier, inc=1, device_id={"proto": peer}, device_id_type=MESH)
    sends = []

    def cols(which):
        return pl.ds(pl.multiple_of(which * share, share), share)

    def rows(which, size):
        return pl.ds(pl.multiple_of(which * size, size), size)

    def dp_move(kind, hop, peer, src, dst):
        return pltpu.make_async_remote_copy(
            src_ref=src, dst_ref=dst, send_sem=dp_send.at[kind, hop], recv_sem=dp_recv.at[kind, hop],
            device_id={"dp": peer}, device_id_type=MESH,
        )

    def pr_move(kind, hop, peer, src, dst):
        return pltpu.make_async_remote_copy(
            src_ref=src, dst_ref=dst, send_sem=pr_send.at[kind, hop], recv_sem=pr_recv.at[kind, hop],
            device_id={"proto": peer}, device_id_type=MESH,
        )

    def start(moves):
        for move in moves:
            move.start()
            sends.append(move)
        return moves

    def arrive(moves):
        for move in moves:
            move.wait_recv()

    own_block = rows(me, own_rows)
    local_moves = [
        pltpu.make_async_copy(tp_ref.at[:, cols(me)], tp_in.at[own_block, :], local_sem.at[0]),
        pltpu.make_async_copy(sp_ref.at[:, cols(me)], sp_in.at[own_block, :], local_sem.at[1]),
    ]
    for move in local_moves:
        move.start()
    t_values = tf_ref[...]
    own_t[...] = t_values / jnp.sqrt(jnp.sum(t_values * t_values, axis=1, keepdims=True) + norm_eps)
    pl.semaphore_wait(barrier, parts - 1 + groups - 1)

    teacher_moves = start(
        [dp_move(0, hop, peer, tp_ref.at[:, cols(peer)], tp_in.at[own_block, :]) for hop, peer in enumerate(dp_peers)]
        + [dp_move(1, hop, peer, own_t, t_in.at[rows(me, teach_rows), :]) for hop, peer in enumerate(dp_peers)]
    )
    t_in[rows(me, teach_rows), :] = own_t[...]

    s_values = sf_ref[...]
    s_norm = jnp.sqrt(jnp.sum(s_values * s_values, axis=1, keepdims=True) + norm_eps)
    s_unit = s_values / s_norm
    teach = lax.broadcasted_iota(jnp.int32, (teach_rows, crop_rows), 0)
    same = crops_t_ref[0:1, :] == teach // GLOBAL_CROPS
    other = crops_t_ref[1:2, :] != teach % GLOBAL_CROPS
    pairs_t = jnp.where(same & other, 1.0, 0.0).astype(f32)
    mixed_at, count_at = crop_rows, crop_rows + teach_rows
    own_s[0:crop_rows, :] = s_unit
    own_s[mixed_at:count_at, :] = dot(pairs_t, s_unit, NN)
    own_s[count_at:, :] = jnp.zeros((SUBLANES, width), f32)
    own_s[count_at:, 0:crop_rows] = jnp.broadcast_to(
        jnp.sum(pairs_t, axis=0, keepdims=True), (SUBLANES, crop_rows)
    )
    s_in[me] = own_s[...]
    for move in local_moves:
        move.wait()

    def first_hop(values, first, kind):
        first[me] = values
        return start(
            [dp_move(kind, hop, peer, first.at[me], first.at[me]) for hop, peer in enumerate(dp_peers)]
        )

    def second_hop(moves, first, second, kind):
        arrive(moves)
        second[mine] = jnp.sum(first[...], axis=0)
        return start(
            [pr_move(kind, hop, peer, second.at[mine], second.at[mine]) for hop, peer in enumerate(pr_peers)]
        )

    def result(moves, second):
        arrive(moves)
        return jnp.sum(jnp.sum(second[...], axis=0), axis=0, keepdims=True)

    def balance(scale):
        values = assign[...]
        if scale is not None:
            values = values * scale
        values = values * (1.0 / jnp.sum(values, axis=1, keepdims=True))
        assign[...] = values
        return fold(values)

    tile = 2 * crop_rows
    half_rows = half * crop_rows

    def place_of(block):
        return (block // 2) + half * lax.rem(block, 2)

    def score_tile(step, carry):
        at = rows(step, tile)
        unit = (unit_hi[...], unit_lo[...])
        expo = jnp.exp(dot3((s_hi[at, :], s_lo[at, :]), unit, NN) / student_temp)
        part = expo[:, 0:LANES]
        for lane in range(1, share // LANES):
            part = part + expo[:, lane * LANES:(lane + 1) * LANES]
        lane_part[at, :] = part
        pieces = split(expo)
        expo_hi[at, :] = pieces[0]
        expo_lo[at, :] = pieces[1]
        return carry

    def f_move(step):
        at = pl.ds(pl.multiple_of((1 - parity) * half_rows + step * tile, tile), tile)
        return dp_move(9, step, partner, f_send.at[at, :], f_pair.at[rows(step, tile), :])

    def feature_tiles(which, near):
        def feature_tile(step, carry):
            at = pl.ds(pl.multiple_of(which * half_rows + step * tile, tile), tile)
            f_send[at, :] = dot3((expo_hi[at, :], expo_lo[at, :]), (unit_hi[...], unit_lo[...]), NT)
            if near:
                f_move(step).start()
            return carry

        lax.fori_loop(0, half // 2, feature_tile, 0)

    arrive(teacher_moves)
    teacher_cols = tp_in[...]
    teacher_norm = jnp.sqrt(jnp.sum(teacher_cols * teacher_cols, axis=0, keepdims=True) + norm_eps)
    assign[...] = jnp.exp(dot((teacher_cols / teacher_norm).T, t_in[...], NT) / temp)
    near = first_hop(balance(None), row_dp.at[0], 4)
    near_move = start([dp_move(3, 0, partner, own_s, s_in.at[me])])
    twin_moves = start([dp_move(3, hop + 1, peer, own_s, s_in.at[me]) for hop, peer in enumerate(twins)])
    near = second_hop(near, row_dp.at[0], row_pr.at[0], 0)
    scale = 1.0 / result(near, row_pr.at[0])
    near = first_hop(balance(scale), row_dp.at[1], 5)
    proto_moves = start(
        [dp_move(2, hop, peer, sp_ref.at[:, cols(peer)], sp_in.at[own_block, :]) for hop, peer in enumerate(dp_peers)]
    )
    arrive(twin_moves)
    onward = start(
        [dp_move(8, hop, partner, s_in.at[block], s_in.at[block]) for hop, block in enumerate(senders)]
    )
    near = second_hop(near, row_dp.at[1], row_pr.at[1], 1)
    arrive(near_move + onward)
    for block in range(parts):
        first = (block // 2 + half * (block % 2)) * crop_rows
        at = slice(first, first + crop_rows)
        crops_now = s_in[block, 0:crop_rows, :]
        high, low = split(crops_now)
        s_hi[at, :] = high
        s_lo[at, :] = low
        count = jnp.broadcast_to(s_in[block, count_at:count_at + 1, :], (LANES, width)).T
        counted[at, :] = crops_now * jnp.concatenate([count[0:crop_rows, :]] * (width // LANES), axis=1)
    counted_t[...] = counted[...].T
    mixed_t[...] = s_in[:, mixed_at:count_at, :].reshape(parts * teach_rows, width).T

    scale = 1.0 / result(near, row_pr.at[1])
    near = first_hop(balance(scale), row_dp.at[2], 6)

    arrive(proto_moves)
    student_cols = sp_in[...]
    student_norm = jnp.sqrt(jnp.sum(student_cols * student_cols, axis=0, keepdims=True) + norm_eps)
    high, low = split(student_cols / student_norm)
    unit_hi[...] = high
    unit_lo[...] = low
    lax.fori_loop(0, half, score_tile, 0)
    tot_near = first_hop(fold(lane_part[...].T), tot_dp, 7)
    near = second_hop(near, row_dp.at[2], row_pr.at[2], 2)
    feature_tiles(1 - parity, True)
    tot_near = second_hop(tot_near, tot_dp, tot_pr, 3)
    feature_tiles(parity, False)
    targets = dot3((unit_hi[...], unit_lo[...]), split(assign[...]), NN)
    scale = 1.0 / result(near, row_pr.at[2])
    mixed_pieces = split(mixed_t[...] * scale)
    g_send[...] = (targets * scale).T
    f_near = [f_move(step) for step in range(half // 2)]
    arrive(f_near)
    sends.extend(f_near)
    own_half = pl.ds(pl.multiple_of(parity * half_rows, half_rows), half_rows)
    f_send[own_half, :] = f_send[own_half, :] + f_pair[...]
    slot = me // 2
    f_moves = start([
        dp_move(10, hop, peer, f_send.at[rows(place_of(peer), crop_rows), :], f_dp.at[slot])
        for hop, peer in enumerate(twins)
    ])
    f_dp[slot] = f_send[rows(place_of(me), crop_rows), :]
    inverse_row = 1.0 / result(tot_near, tot_pr)
    weighted_t = split(counted_t[...] * inverse_row)
    lane_part[...] = jnp.broadcast_to(inverse_row, (LANES, parts * crop_rows)).T

    chunk = share // CHUNKS
    piece_rows = f_part.shape[0] // groups
    back_moves, home_moves = [], []
    for piece in range(CHUNKS):
        at = slice(piece * chunk, (piece + 1) * chunk)
        grad = coef * (
            dot3(weighted_t, (expo_hi[:, at], expo_lo[:, at]), NN)
            - dot3(mixed_pieces, split(assign[at, :]), NT)
        )
        now = sp_in[:, at]
        norm = jnp.sqrt(jnp.sum(now * now, axis=0, keepdims=True) + norm_eps)
        unit = now / norm
        proto_grad = (grad - unit * jnp.sum(unit * grad, axis=0, keepdims=True)) / norm
        square = jnp.sum(proto_grad * proto_grad, axis=0, keepdims=True) / width
        moved[:, at] = proto_grad / jnp.sqrt(square + square_eps)
        place = pl.ds(pl.multiple_of(me * share + piece * chunk, chunk), chunk)
        back_moves += start([
            dp_move(12 + piece, hop, peer, moved.at[rows(peer, own_rows), at], step_ref.at[:, place])
            for hop, peer in enumerate(dp_peers)
        ])
        home_moves.append(pltpu.make_async_copy(moved.at[own_block, at], step_ref.at[:, place], local_sem.at[2 + piece]))
        home_moves[-1].start()
        if piece == 0:
            g_moves = start([
                dp_move(11, hop, peer, g_send.at[rows(peer, teach_rows), :], g_dp.at[me])
                for hop, peer in enumerate(dp_peers)
            ])
            g_dp[me] = g_send[rows(me, teach_rows), :]
        if piece == 1:
            arrive(f_moves)
            f_part[0:crop_rows, :] = jnp.sum(f_dp[...], axis=0)
            if f_part.shape[0] > crop_rows:
                f_part[crop_rows:, :] = jnp.zeros((f_part.shape[0] - crop_rows, width), f32)
            f_across = start([
                pr_move(4, hop, peer, f_part.at[rows(peer, piece_rows), :], f_pr.at[mine])
                for hop, peer in enumerate(pr_peers)
            ])
            f_pr[mine] = f_part[rows(mine, piece_rows), :]
    arrive(f_across)
    own_piece = rows(mine, piece_rows)
    f_sum[own_piece, :] = jnp.sum(f_pr[...], axis=0)
    f_last = start(
        [pr_move(6, hop, peer, f_sum.at[own_piece, :], f_sum.at[own_piece, :]) for hop, peer in enumerate(pr_peers)]
    )
    arrive(g_moves)
    g_pr[mine] = jnp.sum(g_dp[...], axis=0)
    g_across = start(
        [pr_move(5, hop, peer, g_pr.at[mine], g_pr.at[mine]) for hop, peer in enumerate(pr_peers)]
    )
    teach = lax.broadcasted_iota(jnp.int32, (crop_rows, teach_rows), 1)
    same = crops_ref[:, 0:1] == teach // GLOBAL_CROPS
    other = crops_ref[:, 1:2] != teach % GLOBAL_CROPS
    pairs = jnp.where(same & other, 1.0, 0.0).astype(f32)
    count = jnp.sum(pairs, axis=1, keepdims=True)
    inverse = jnp.concatenate([lane_part[rows(place_of(me), crop_rows), :]] * (width // LANES), axis=1)
    s_values = sf_ref[...]
    s_norm = jnp.sqrt(jnp.sum(s_values * s_values, axis=1, keepdims=True) + norm_eps)
    s_unit = s_values / s_norm
    arrive(g_across)
    wanted = dot(pairs, jnp.sum(g_pr[...], axis=0), NN)
    arrive(f_last)
    feature_unit = coef * (count * (f_sum[0:crop_rows, :] * inverse) - wanted)
    fgrad_ref[...] = (
        feature_unit - s_unit * jnp.sum(s_unit * feature_unit, axis=1, keepdims=True)
    ) / s_norm
    arrive(back_moves)
    for move in home_moves:
        move.wait()
    for move in sends:
        move.wait_send()


def body(student_feats, teacher_feats, student_proto, teacher_proto, crops, step):
    parts, groups = lax.axis_size("dp"), lax.axis_size("proto")
    crop_rows, width = student_feats.shape
    teach_rows = teacher_feats.shape[0]
    own_rows, columns = student_proto.shape
    share = columns // parts
    images = teach_rows // GLOBAL_CROPS * parts
    pair_total = GLOBAL_CROPS * (GLOBAL_CROPS - 1) + (CROPS - GLOBAL_CROPS) * GLOBAL_CROPS
    coef = loss_scale / (pair_total * images * student_temp)
    all_s, all_t = parts * crop_rows, parts * teach_rows
    packed = crop_rows + teach_rows + SUBLANES
    kinds = 12 + CHUNKS
    piece_rows = -(-crop_rows // (groups * SUBLANES)) * SUBLANES
    rate, teacher_temp, momentum = plan(step)

    def vmem(*shape, dtype=f32):
        return pltpu.VMEM(shape, dtype)

    def sems(*shape):
        return pltpu.SemaphoreType.DMA(shape)

    whole, outside = pl.BlockSpec(memory_space=pltpu.VMEM), pl.BlockSpec(memory_space=pl.ANY)
    shapes = [student_proto, student_feats]
    direction, feature_grad = pl.pallas_call(
        functools.partial(kernel, parts, groups, coef),
        out_shape=[jax.ShapeDtypeStruct(one.shape, f32) for one in shapes],
        in_specs=[pl.BlockSpec(memory_space=pltpu.SMEM), whole, whole, outside, outside, whole, whole],
        out_specs=[outside, whole],
        scratch_shapes=[
            vmem(width, share), vmem(width, share),
            vmem(parts, packed, width), vmem(all_t, width),
            vmem(packed, width), vmem(teach_rows, width),
            vmem(width, share, dtype=bf16), vmem(width, share, dtype=bf16),
            vmem(all_s, share, dtype=bf16), vmem(all_s, share, dtype=bf16),
            vmem(all_s, width, dtype=bf16), vmem(all_s, width, dtype=bf16),
            vmem(all_s, LANES), vmem(all_s, width), vmem(width, all_s), vmem(width, all_t),
            vmem(share, all_t),
            vmem(ITERS, parts, SUBLANES, all_t), vmem(ITERS, groups, SUBLANES, all_t),
            vmem(parts, SUBLANES, all_s), vmem(groups, SUBLANES, all_s),
            vmem(all_s, width), vmem(all_s // 2, width),
            vmem(parts // 2, crop_rows, width), vmem(groups * piece_rows, width),
            vmem(groups, piece_rows, width), vmem(groups * piece_rows, width),
            vmem(all_t, width), vmem(parts, teach_rows, width), vmem(groups, teach_rows, width),
            vmem(width, share),
            sems(kinds, parts), sems(kinds, parts), sems(7, groups), sems(7, groups), sems(2 + CHUNKS),
        ],
        compiler_params=pltpu.CompilerParams(
            collective_id=0, has_side_effects=True, vmem_limit_bytes=56 * 1024 * 1024
        ),
    )(jnp.stack([rate, teacher_temp]), student_feats, teacher_feats, student_proto, teacher_proto, crops, crops.T)
    student_next = student_proto - rate * (direction + weight_decay * student_proto)
    teacher_next = momentum * teacher_proto + (1.0 - momentum) * student_next
    return (student_next, teacher_next, feature_grad)


def solution(mesh):
    in_specs = (
        P("dp", None),
        P("dp", None),
        P("dp", "proto"),
        P("dp", "proto"),
        P("dp", None),
        P(),
    )
    out_specs = (P("dp", "proto"), P("dp", "proto"), P("dp", None))
    return jax.shard_map(body, mesh=mesh, in_specs=in_specs, out_specs=out_specs, check_vma=False)
```

```python
import functools

import jax
import jax.numpy as jnp
from jax import lax
from jax.experimental import pallas as pl
from jax.experimental.pallas import tpu as pltpu
from jax.sharding import PartitionSpec as P

CROPS = 10
GLOBAL_CROPS = 2
ITERS = 3
WARM_STEPS = 12500
TOTAL_STEPS = 625000


student_temp = 0.1
loss_scale = 16777216.0
norm_eps = 1e-06
square_eps = 1e-06
rate_peak = 0.05
weight_decay = 0.04
momentum_base = 0.994
highest = lax.Precision.HIGHEST


def plan(step):
    value = step[0].astype(jnp.float32)
    ramp = jnp.minimum(1.0, value / WARM_STEPS)
    rate = rate_peak * (0.25 + 0.75 * ramp)
    teacher_temp = 0.04 + 0.03 * ramp
    momentum = 1.0 - (1.0 - momentum_base) * (jnp.cos(jnp.pi * value / TOTAL_STEPS) + 1.0) * 0.5
    return (rate, teacher_temp, momentum)


NN = (((1,), (0,)), ((), ()))
NT = (((1,), (1,)), ((), ()))
MESH = pl.DeviceIdType.MESH
LANES = 128
SUBLANES = 8
CHUNKS = 4
f32 = jnp.float32
bf16 = jnp.bfloat16


def dot(left, right, dims):
    return lax.dot_general(left, right, dims, precision=highest, preferred_element_type=f32)


def split(values):
    high = values.astype(bf16)
    return high, (values - high.astype(f32)).astype(bf16)


def dot3(left, right, dims):
    def one(a, b):
        return lax.dot_general(a, b, dims, preferred_element_type=f32)

    return one(left[0], right[0]) + (one(left[0], right[1]) + one(left[1], right[0]))


def fold(values):
    return jnp.sum(values, axis=0, keepdims=True)


def kernel(
    parts, groups, coef,
    plan_ref, sf_ref, tf_ref, sp_ref, tp_ref, crops_ref, crops_t_ref,
    step_ref, fgrad_ref,
    sp_in, tp_in, s_in, t_in, own_s, own_t, unit_hi, unit_lo, expo_hi, expo_lo,
    s_hi, s_lo, lane_part, counted, counted_t, mixed_t, assign, row_dp, row_pr, tot_dp, tot_pr,
    inv_norm, f_send, f_pair, f_dp, f_part, f_pr, f_sum, g_send, g_dp, g_pr, moved,
    dp_send, dp_recv, pr_send, pr_recv, local_sem,
):
    me, mine = lax.axis_index("dp"), lax.axis_index("proto")
    crop_rows, width = sf_ref.shape
    teach_rows = tf_ref.shape[0]
    own_rows, columns = sp_ref.shape
    share = columns // parts
    half = parts // 2
    temp = plan_ref[1]
    parity = lax.rem(me, 2)
    partner = me + 1 - 2 * parity
    twins = [lax.rem(me + 2 * hop, parts) for hop in range(1, half)]
    senders = [lax.rem(me + parts - 2 * hop, parts) for hop in range(1, half)]
    dp_peers = [lax.rem(me + hop, parts) for hop in range(1, parts)]
    pr_peers = [lax.rem(mine + hop, groups) for hop in range(1, groups)]
    barrier = pltpu.get_barrier_semaphore()
    for peer in dp_peers:
        pl.semaphore_signal(barrier, inc=1, device_id={"dp": peer}, device_id_type=MESH)
    for peer in pr_peers:
        pl.semaphore_signal(barrier, inc=1, device_id={"proto": peer}, device_id_type=MESH)
    sends = []

    def cols(which):
        return pl.ds(pl.multiple_of(which * share, share), share)

    def rows(which, size):
        return pl.ds(pl.multiple_of(which * size, size), size)

    def dp_move(kind, hop, peer, src, dst):
        return pltpu.make_async_remote_copy(
            src_ref=src, dst_ref=dst, send_sem=dp_send.at[kind, hop], recv_sem=dp_recv.at[kind, hop],
            device_id={"dp": peer}, device_id_type=MESH,
        )

    def pr_move(kind, hop, peer, src, dst):
        return pltpu.make_async_remote_copy(
            src_ref=src, dst_ref=dst, send_sem=pr_send.at[kind, hop], recv_sem=pr_recv.at[kind, hop],
            device_id={"proto": peer}, device_id_type=MESH,
        )

    def start(moves):
        for move in moves:
            move.start()
            sends.append(move)
        return moves

    def arrive(moves):
        for move in moves:
            move.wait_recv()

    own_block = rows(me, own_rows)
    local_moves = [
        pltpu.make_async_copy(tp_ref.at[:, cols(me)], tp_in.at[own_block, :], local_sem.at[0]),
        pltpu.make_async_copy(sp_ref.at[:, cols(me)], sp_in.at[own_block, :], local_sem.at[1]),
    ]
    for move in local_moves:
        move.start()
    t_values = tf_ref[...]
    own_t[...] = t_values / jnp.sqrt(jnp.sum(t_values * t_values, axis=1, keepdims=True) + norm_eps)
    pl.semaphore_wait(barrier, parts - 1 + groups - 1)

    teacher_moves = start(
        [dp_move(0, hop, peer, tp_ref.at[:, cols(peer)], tp_in.at[own_block, :]) for hop, peer in enumerate(dp_peers)]
        + [dp_move(1, hop, peer, own_t, t_in.at[rows(me, teach_rows), :]) for hop, peer in enumerate(dp_peers)]
    )
    t_in[rows(me, teach_rows), :] = own_t[...]

    s_values = sf_ref[...]
    s_norm = jnp.sqrt(jnp.sum(s_values * s_values, axis=1, keepdims=True) + norm_eps)
    s_unit = s_values / s_norm
    teach = lax.broadcasted_iota(jnp.int32, (teach_rows, crop_rows), 0)
    same = crops_t_ref[0:1, :] == teach // GLOBAL_CROPS
    other = crops_t_ref[1:2, :] != teach % GLOBAL_CROPS
    pairs_t = jnp.where(same & other, 1.0, 0.0).astype(f32)
    mixed_at, count_at = crop_rows, crop_rows + teach_rows
    own_s[0:crop_rows, :] = s_unit
    own_s[mixed_at:count_at, :] = dot(pairs_t, s_unit, NN)
    own_s[count_at:, :] = jnp.zeros((SUBLANES, width), f32)
    own_s[count_at:, 0:crop_rows] = jnp.broadcast_to(
        jnp.sum(pairs_t, axis=0, keepdims=True), (SUBLANES, crop_rows)
    )
    s_in[me] = own_s[...]
    for move in local_moves:
        move.wait()

    def first_hop(values, first, kind):
        first[me] = values
        return start(
            [dp_move(kind, hop, peer, first.at[me], first.at[me]) for hop, peer in enumerate(dp_peers)]
        )

    def second_hop(moves, first, second, kind):
        arrive(moves)
        second[mine] = jnp.sum(first[...], axis=0)
        return start(
            [pr_move(kind, hop, peer, second.at[mine], second.at[mine]) for hop, peer in enumerate(pr_peers)]
        )

    def result(moves, second):
        arrive(moves)
        return jnp.sum(second[...], axis=0)

    def balance(scale):
        values = assign[...]
        if scale is not None:
            values = values * scale
        values = values * (1.0 / jnp.sum(values, axis=1, keepdims=True))
        assign[...] = values
        return fold(values)

    tile = 2 * crop_rows
    half_rows = half * crop_rows

    def place_of(block):
        return (block // 2) + half * lax.rem(block, 2)

    def score_tile(step, carry):
        at = rows(step, tile)
        unit = (unit_hi[...], unit_lo[...])
        expo = jnp.exp(dot3((s_hi[at, :], s_lo[at, :]), unit, NN) / student_temp)
        part = expo[:, 0:LANES]
        for lane in range(1, share // LANES):
            part = part + expo[:, lane * LANES:(lane + 1) * LANES]
        lane_part[at, :] = part
        pieces = split(expo)
        expo_hi[at, :] = pieces[0]
        expo_lo[at, :] = pieces[1]
        return carry

    def f_move(step):
        at = pl.ds(pl.multiple_of((1 - parity) * half_rows + step * tile, tile), tile)
        return dp_move(9, step, partner, f_send.at[at, :], f_pair.at[rows(step, tile), :])

    def feature_tiles(which, near):
        def feature_tile(step, carry):
            at = pl.ds(pl.multiple_of(which * half_rows + step * tile, tile), tile)
            f_send[at, :] = dot3((expo_hi[at, :], expo_lo[at, :]), (unit_hi[...], unit_lo[...]), NT)
            if near:
                f_move(step).start()
            return carry

        lax.fori_loop(0, half // 2, feature_tile, 0)

    arrive(teacher_moves)
    teacher_cols = tp_in[...]
    inverse = 1.0 / jnp.sqrt(jnp.sum(teacher_cols * teacher_cols, axis=0, keepdims=True) + norm_eps)
    assign[...] = jnp.exp(dot((teacher_cols * inverse).T, t_in[...], NT) * (1.0 / temp))
    near = first_hop(balance(None), row_dp.at[0], 4)
    near_move = start([dp_move(3, 0, partner, own_s, s_in.at[me])])
    twin_moves = start([dp_move(3, hop + 1, peer, own_s, s_in.at[me]) for hop, peer in enumerate(twins)])
    near = second_hop(near, row_dp.at[0], row_pr.at[0], 0)
    scale = 1.0 / result(near, row_pr.at[0])
    near = first_hop(balance(scale), row_dp.at[1], 5)
    proto_moves = start(
        [dp_move(2, hop, peer, sp_ref.at[:, cols(peer)], sp_in.at[own_block, :]) for hop, peer in enumerate(dp_peers)]
    )
    arrive(twin_moves)
    onward = start(
        [dp_move(8, hop, partner, s_in.at[block], s_in.at[block]) for hop, block in enumerate(senders)]
    )
    near = second_hop(near, row_dp.at[1], row_pr.at[1], 1)
    arrive(near_move + onward)
    for block in range(parts):
        first = (block // 2 + half * (block % 2)) * crop_rows
        at = slice(first, first + crop_rows)
        crops_now = s_in[block, 0:crop_rows, :]
        high, low = split(crops_now)
        s_hi[at, :] = high
        s_lo[at, :] = low
        count = jnp.broadcast_to(s_in[block, count_at:count_at + 1, :], (LANES, width)).T
        counted[at, :] = crops_now * jnp.concatenate([count[0:crop_rows, :]] * (width // LANES), axis=1)
    counted_t[...] = counted[...].T
    mixed_t[...] = s_in[:, mixed_at:count_at, :].reshape(parts * teach_rows, width).T

    scale = 1.0 / result(near, row_pr.at[1])
    near = first_hop(balance(scale), row_dp.at[2], 6)

    arrive(proto_moves)
    student_cols = sp_in[...]
    inverse = 1.0 / jnp.sqrt(jnp.sum(student_cols * student_cols, axis=0, keepdims=True) + norm_eps)
    inv_norm[...] = jnp.broadcast_to(inverse, inv_norm.shape)
    high, low = split(student_cols * inverse)
    unit_hi[...] = high
    unit_lo[...] = low
    lax.fori_loop(0, half, score_tile, 0)
    tot_near = first_hop(fold(lane_part[...].T), tot_dp, 7)
    near = second_hop(near, row_dp.at[2], row_pr.at[2], 2)
    feature_tiles(1 - parity, True)
    tot_near = second_hop(tot_near, tot_dp, tot_pr, 3)
    feature_tiles(parity, False)
    targets = dot3((unit_hi[...], unit_lo[...]), split(assign[...]), NN)
    scale = 1.0 / result(near, row_pr.at[2])
    mixed_pieces = split(mixed_t[...] * scale)
    g_send[...] = (targets * scale).T
    g_moves = start([
        dp_move(11, hop, peer, g_send.at[rows(peer, teach_rows), :], g_dp.at[me])
        for hop, peer in enumerate(dp_peers)
    ])
    g_dp[me] = g_send[rows(me, teach_rows), :]
    f_near = [f_move(step) for step in range(half // 2)]
    arrive(f_near)
    sends.extend(f_near)
    own_half = pl.ds(pl.multiple_of(parity * half_rows, half_rows), half_rows)
    f_send[own_half, :] = f_send[own_half, :] + f_pair[...]
    slot = me // 2
    f_moves = start([
        dp_move(10, hop, peer, f_send.at[rows(place_of(peer), crop_rows), :], f_dp.at[slot])
        for hop, peer in enumerate(twins)
    ])
    f_dp[slot] = f_send[rows(place_of(me), crop_rows), :]
    inverse_row = 1.0 / result(tot_near, tot_pr)
    weighted_t = split(counted_t[...] * inverse_row)
    lane_part[...] = jnp.broadcast_to(inverse_row, (LANES, parts * crop_rows)).T

    chunk = share // CHUNKS
    piece_rows = f_part.shape[0] // groups
    back_moves, home_moves = [], []
    for piece in range(CHUNKS):
        at = slice(piece * chunk, (piece + 1) * chunk)
        grad = coef * (
            dot3(weighted_t, (expo_hi[:, at], expo_lo[:, at]), NN)
            - dot3(mixed_pieces, split(assign[at, :]), NT)
        )
        now = sp_in[:, at]
        inverse = inv_norm[0:1, at]
        unit = now * inverse
        proto_grad = (grad - unit * jnp.sum(unit * grad, axis=0, keepdims=True)) * inverse
        square = jnp.sum(proto_grad * proto_grad, axis=0, keepdims=True) / width
        moved[:, at] = proto_grad * (1.0 / jnp.sqrt(square + square_eps))
        place = pl.ds(pl.multiple_of(me * share + piece * chunk, chunk), chunk)
        back_moves += start([
            dp_move(12 + piece, hop, peer, moved.at[rows(peer, own_rows), at], step_ref.at[:, place])
            for hop, peer in enumerate(dp_peers)
        ])
        home_moves.append(pltpu.make_async_copy(moved.at[own_block, at], step_ref.at[:, place], local_sem.at[2 + piece]))
        home_moves[-1].start()
        if piece == 1:
            arrive(f_moves)
            f_part[0:crop_rows, :] = jnp.sum(f_dp[...], axis=0)
            if f_part.shape[0] > crop_rows:
                f_part[crop_rows:, :] = jnp.zeros((f_part.shape[0] - crop_rows, width), f32)
            f_across = start([
                pr_move(4, hop, peer, f_part.at[rows(peer, piece_rows), :], f_pr.at[mine])
                for hop, peer in enumerate(pr_peers)
            ])
            f_pr[mine] = f_part[rows(mine, piece_rows), :]
    arrive(f_across)
    own_piece = rows(mine, piece_rows)
    f_sum[own_piece, :] = jnp.sum(f_pr[...], axis=0)
    f_last = start(
        [pr_move(6, hop, peer, f_sum.at[own_piece, :], f_sum.at[own_piece, :]) for hop, peer in enumerate(pr_peers)]
    )
    arrive(g_moves)
    g_pr[mine] = jnp.sum(g_dp[...], axis=0)
    g_across = start(
        [pr_move(5, hop, peer, g_pr.at[mine], g_pr.at[mine]) for hop, peer in enumerate(pr_peers)]
    )
    teach = lax.broadcasted_iota(jnp.int32, (crop_rows, teach_rows), 1)
    same = crops_ref[:, 0:1] == teach // GLOBAL_CROPS
    other = crops_ref[:, 1:2] != teach % GLOBAL_CROPS
    pairs = jnp.where(same & other, 1.0, 0.0).astype(f32)
    count = jnp.sum(pairs, axis=1, keepdims=True)
    inverse = jnp.concatenate([lane_part[rows(place_of(me), crop_rows), :]] * (width // LANES), axis=1)
    s_values = sf_ref[...]
    s_norm = jnp.sqrt(jnp.sum(s_values * s_values, axis=1, keepdims=True) + norm_eps)
    s_unit = s_values / s_norm
    arrive(g_across)
    wanted = dot(pairs, jnp.sum(g_pr[...], axis=0), NN)
    arrive(f_last)
    feature_unit = coef * (count * (f_sum[0:crop_rows, :] * inverse) - wanted)
    fgrad_ref[...] = (
        feature_unit - s_unit * jnp.sum(s_unit * feature_unit, axis=1, keepdims=True)
    ) / s_norm
    arrive(back_moves)
    for move in home_moves:
        move.wait()
    for move in sends:
        move.wait_send()


def body(student_feats, teacher_feats, student_proto, teacher_proto, crops, step):
    parts, groups = lax.axis_size("dp"), lax.axis_size("proto")
    crop_rows, width = student_feats.shape
    teach_rows = teacher_feats.shape[0]
    own_rows, columns = student_proto.shape
    share = columns // parts
    images = teach_rows // GLOBAL_CROPS * parts
    pair_total = GLOBAL_CROPS * (GLOBAL_CROPS - 1) + (CROPS - GLOBAL_CROPS) * GLOBAL_CROPS
    coef = loss_scale / (pair_total * images * student_temp)
    all_s, all_t = parts * crop_rows, parts * teach_rows
    packed = crop_rows + teach_rows + SUBLANES
    kinds = 12 + CHUNKS
    piece_rows = -(-crop_rows // (groups * SUBLANES)) * SUBLANES
    rate, teacher_temp, momentum = plan(step)

    def vmem(*shape, dtype=f32):
        return pltpu.VMEM(shape, dtype)

    def sems(*shape):
        return pltpu.SemaphoreType.DMA(shape)

    whole, outside = pl.BlockSpec(memory_space=pltpu.VMEM), pl.BlockSpec(memory_space=pl.ANY)
    shapes = [student_proto, student_feats]
    direction, feature_grad = pl.pallas_call(
        functools.partial(kernel, parts, groups, coef),
        out_shape=[jax.ShapeDtypeStruct(one.shape, f32) for one in shapes],
        in_specs=[pl.BlockSpec(memory_space=pltpu.SMEM), whole, whole, outside, outside, whole, whole],
        out_specs=[outside, whole],
        scratch_shapes=[
            vmem(width, share), vmem(width, share),
            vmem(parts, packed, width), vmem(all_t, width),
            vmem(packed, width), vmem(teach_rows, width),
            vmem(width, share, dtype=bf16), vmem(width, share, dtype=bf16),
            vmem(all_s, share, dtype=bf16), vmem(all_s, share, dtype=bf16),
            vmem(all_s, width, dtype=bf16), vmem(all_s, width, dtype=bf16),
            vmem(all_s, LANES), vmem(all_s, width), vmem(width, all_s), vmem(width, all_t),
            vmem(share, all_t),
            vmem(ITERS, parts, 1, all_t), vmem(ITERS, groups, 1, all_t),
            vmem(parts, 1, all_s), vmem(groups, 1, all_s),
            vmem(SUBLANES, share), vmem(all_s, width), vmem(all_s // 2, width),
            vmem(parts // 2, crop_rows, width), vmem(groups * piece_rows, width),
            vmem(groups, piece_rows, width), vmem(groups * piece_rows, width),
            vmem(all_t, width), vmem(parts, teach_rows, width), vmem(groups, teach_rows, width),
            vmem(width, share),
            sems(kinds, parts), sems(kinds, parts), sems(7, groups), sems(7, groups), sems(2 + CHUNKS),
        ],
        compiler_params=pltpu.CompilerParams(
            collective_id=0, has_side_effects=True, vmem_limit_bytes=56 * 1024 * 1024
        ),
    )(jnp.stack([rate, teacher_temp]), student_feats, teacher_feats, student_proto, teacher_proto, crops, crops.T)
    student_next = student_proto - rate * (direction + weight_decay * student_proto)
    teacher_next = momentum * teacher_proto + (1.0 - momentum) * student_next
    return (student_next, teacher_next, feature_grad)


def solution(mesh):
    in_specs = (
        P("dp", None),
        P("dp", None),
        P("dp", "proto"),
        P("dp", "proto"),
        P("dp", None),
        P(),
    )
    out_specs = (P("dp", "proto"), P("dp", "proto"), P("dp", None))
    return jax.shard_map(body, mesh=mesh, in_specs=in_specs, out_specs=out_specs, check_vma=False)
```

```python
import functools

import jax
import jax.numpy as jnp
from jax import lax
from jax.experimental import pallas as pl
from jax.experimental.pallas import tpu as pltpu
from jax.sharding import PartitionSpec as P

CROPS = 10
GLOBAL_CROPS = 2
ITERS = 3
WARM_STEPS = 12500
TOTAL_STEPS = 625000


student_temp = 0.1
loss_scale = 16777216.0
norm_eps = 1e-06
square_eps = 1e-06
rate_peak = 0.05
weight_decay = 0.04
momentum_base = 0.994
highest = lax.Precision.HIGHEST


def plan(step):
    value = step[0].astype(jnp.float32)
    ramp = jnp.minimum(1.0, value / WARM_STEPS)
    rate = rate_peak * (0.25 + 0.75 * ramp)
    teacher_temp = 0.04 + 0.03 * ramp
    momentum = 1.0 - (1.0 - momentum_base) * (jnp.cos(jnp.pi * value / TOTAL_STEPS) + 1.0) * 0.5
    return (rate, teacher_temp, momentum)


NN = (((1,), (0,)), ((), ()))
NT = (((1,), (1,)), ((), ()))
MESH = pl.DeviceIdType.MESH
LANES = 128
SUBLANES = 8
CHUNKS = 4
f32 = jnp.float32
bf16 = jnp.bfloat16


def dot(left, right, dims):
    return lax.dot_general(left, right, dims, precision=highest, preferred_element_type=f32)


def split(values):
    high = values.astype(bf16)
    return high, (values - high.astype(f32)).astype(bf16)


def dot3(left, right, dims):
    def one(a, b):
        return lax.dot_general(a, b, dims, preferred_element_type=f32)

    return one(left[0], right[0]) + (one(left[0], right[1]) + one(left[1], right[0]))


def fold(values):
    return jnp.sum(values, axis=0, keepdims=True)


def kernel(
    parts, groups, coef,
    plan_ref, sf_ref, tf_ref, sp_ref, tp_ref, crops_ref,
    step_ref, fgrad_ref,
    sp_in, tp_in, s_in, t_in, own_s, own_t, unit_hi, unit_lo, expo_hi, expo_lo,
    s_hi, s_lo, lane_part, counted, counted_t, mixed_t, assign, row_dp, row_pr, tot_dp, tot_pr,
    pair_pad, inv_norm, f_send, f_pair, f_dp, f_part, f_pr, f_sum, g_send, g_dp, g_pr, moved,
    dp_send, dp_recv, pr_send, pr_recv, local_sem,
):
    me, mine = lax.axis_index("dp"), lax.axis_index("proto")
    crop_rows, width = sf_ref.shape
    teach_rows = tf_ref.shape[0]
    own_rows, columns = sp_ref.shape
    share = columns // parts
    half = parts // 2
    temp = 0.04 + 0.03 * jnp.minimum(1.0, plan_ref[0].astype(f32) / WARM_STEPS)
    parity = lax.rem(me, 2)
    partner = me + 1 - 2 * parity
    twins = [lax.rem(me + 2 * hop, parts) for hop in range(1, half)]
    senders = [lax.rem(me + parts - 2 * hop, parts) for hop in range(1, half)]
    dp_peers = [lax.rem(me + hop, parts) for hop in range(1, parts)]
    pr_peers = [lax.rem(mine + hop, groups) for hop in range(1, groups)]
    barrier = pltpu.get_barrier_semaphore()
    for peer in dp_peers:
        pl.semaphore_signal(barrier, inc=1, device_id={"dp": peer}, device_id_type=MESH)
    for peer in pr_peers:
        pl.semaphore_signal(barrier, inc=1, device_id={"proto": peer}, device_id_type=MESH)
    sends = []

    def cols(which):
        return pl.ds(pl.multiple_of(which * share, share), share)

    def rows(which, size):
        return pl.ds(pl.multiple_of(which * size, size), size)

    def dp_move(kind, hop, peer, src, dst):
        return pltpu.make_async_remote_copy(
            src_ref=src, dst_ref=dst, send_sem=dp_send.at[kind, hop], recv_sem=dp_recv.at[kind, hop],
            device_id={"dp": peer}, device_id_type=MESH,
        )

    def pr_move(kind, hop, peer, src, dst):
        return pltpu.make_async_remote_copy(
            src_ref=src, dst_ref=dst, send_sem=pr_send.at[kind, hop], recv_sem=pr_recv.at[kind, hop],
            device_id={"proto": peer}, device_id_type=MESH,
        )

    def start(moves):
        for move in moves:
            move.start()
            sends.append(move)
        return moves

    def arrive(moves):
        for move in moves:
            move.wait_recv()

    own_block = rows(me, own_rows)
    local_moves = [
        pltpu.make_async_copy(tp_ref.at[:, cols(me)], tp_in.at[own_block, :], local_sem.at[0]),
        pltpu.make_async_copy(sp_ref.at[:, cols(me)], sp_in.at[own_block, :], local_sem.at[1]),
    ]
    for move in local_moves:
        move.start()
    t_values = tf_ref[...]
    own_t[...] = t_values / jnp.sqrt(jnp.sum(t_values * t_values, axis=1, keepdims=True) + norm_eps)
    pl.semaphore_wait(barrier, parts - 1 + groups - 1)

    teacher_moves = start(
        [dp_move(0, hop, peer, tp_ref.at[:, cols(peer)], tp_in.at[own_block, :]) for hop, peer in enumerate(dp_peers)]
        + [dp_move(1, hop, peer, own_t, t_in.at[rows(me, teach_rows), :]) for hop, peer in enumerate(dp_peers)]
    )
    t_in[rows(me, teach_rows), :] = own_t[...]

    s_values = sf_ref[...]
    s_norm = jnp.sqrt(jnp.sum(s_values * s_values, axis=1, keepdims=True) + norm_eps)
    s_unit = s_values / s_norm
    teach = lax.broadcasted_iota(jnp.int32, (crop_rows, pair_pad.shape[1]), 1)
    same = crops_ref[:, 0:1] == teach // GLOBAL_CROPS
    other = crops_ref[:, 1:2] != teach % GLOBAL_CROPS
    pair_pad[...] = jnp.zeros(pair_pad.shape, f32)
    pair_pad[0:crop_rows, :] = jnp.where(same & other & (teach < teach_rows), 1.0, 0.0).astype(f32)
    pairs_t = pair_pad[...].T[0:teach_rows, 0:crop_rows]
    mixed_at, count_at = crop_rows, crop_rows + teach_rows
    own_s[0:crop_rows, :] = s_unit
    own_s[mixed_at:count_at, :] = dot(pairs_t, s_unit, NN)
    own_s[count_at:, :] = jnp.zeros((SUBLANES, width), f32)
    own_s[count_at:, 0:crop_rows] = jnp.broadcast_to(
        jnp.sum(pairs_t, axis=0, keepdims=True), (SUBLANES, crop_rows)
    )
    s_in[me] = own_s[...]
    for move in local_moves:
        move.wait()

    def first_hop(values, first, kind):
        first[me] = values
        return start(
            [dp_move(kind, hop, peer, first.at[me], first.at[me]) for hop, peer in enumerate(dp_peers)]
        )

    def second_hop(moves, first, second, kind):
        arrive(moves)
        second[mine] = jnp.sum(first[...], axis=0)
        return start(
            [pr_move(kind, hop, peer, second.at[mine], second.at[mine]) for hop, peer in enumerate(pr_peers)]
        )

    def result(moves, second):
        arrive(moves)
        return jnp.sum(second[...], axis=0)

    def balance(scale):
        values = assign[...]
        if scale is not None:
            values = values * scale
        values = values * (1.0 / jnp.sum(values, axis=1, keepdims=True))
        assign[...] = values
        return fold(values)

    tile = 2 * crop_rows
    half_rows = half * crop_rows

    def place_of(block):
        return (block // 2) + half * lax.rem(block, 2)

    def scores(side):
        at_cols = slice(side * wide, (side + 1) * wide)
        arrive(proto_moves[side])
        now = sp_in[:, at_cols]
        inverse = 1.0 / jnp.sqrt(jnp.sum(now * now, axis=0, keepdims=True) + norm_eps)
        inv_norm[:, at_cols] = jnp.broadcast_to(inverse, (SUBLANES, wide))
        high, low = split(now * inverse)
        unit_hi[:, at_cols] = high
        unit_lo[:, at_cols] = low

        def score_tile(step, carry):
            at = rows(step, tile)
            unit = (unit_hi[:, at_cols], unit_lo[:, at_cols])
            expo = jnp.exp(dot3((s_hi[at, :], s_lo[at, :]), unit, NN) * (1.0 / student_temp))
            part = expo[:, 0:LANES]
            for lane in range(1, wide // LANES):
                part = part + expo[:, lane * LANES:(lane + 1) * LANES]
            lane_part[at, :] = part if side == 0 else lane_part[at, :] + part
            pieces = split(expo)
            expo_hi[at, at_cols] = pieces[0]
            expo_lo[at, at_cols] = pieces[1]
            return carry

        lax.fori_loop(0, half, score_tile, 0)

    def f_move(step):
        at = pl.ds(pl.multiple_of((1 - parity) * half_rows + step * tile, tile), tile)
        return dp_move(9, step, partner, f_send.at[at, :], f_pair.at[rows(step, tile), :])

    def feature_tiles(which, near):
        def feature_tile(step, carry):
            at = pl.ds(pl.multiple_of(which * half_rows + step * tile, tile), tile)
            f_send[at, :] = dot3((expo_hi[at, :], expo_lo[at, :]), (unit_hi[...], unit_lo[...]), NT)
            if near:
                f_move(step).start()
            return carry

        lax.fori_loop(0, half // 2, feature_tile, 0)

    arrive(teacher_moves)
    teacher_cols = tp_in[...]
    inverse = 1.0 / jnp.sqrt(jnp.sum(teacher_cols * teacher_cols, axis=0, keepdims=True) + norm_eps)
    assign[...] = jnp.exp(dot((teacher_cols * inverse).T, t_in[...], NT) * (1.0 / temp))
    near = first_hop(balance(None), row_dp.at[0], 4)
    near_move = start([dp_move(3, 0, partner, own_s, s_in.at[me])])
    twin_moves = start([dp_move(3, hop + 1, peer, own_s, s_in.at[me]) for hop, peer in enumerate(twins)])
    near = second_hop(near, row_dp.at[0], row_pr.at[0], 0)
    scale = 1.0 / result(near, row_pr.at[0])
    near = first_hop(balance(scale), row_dp.at[1], 5)
    wide = share // 2
    proto_moves = []
    for side in range(2):
        proto_moves.append(start([
            dp_move(
                (2, 12 + CHUNKS)[side], hop, peer,
                sp_ref.at[:, pl.ds(pl.multiple_of(peer * share + side * wide, wide), wide)],
                sp_in.at[own_block, side * wide:(side + 1) * wide],
            )
            for hop, peer in enumerate(dp_peers)
        ]))
    arrive(twin_moves)
    onward = start(
        [dp_move(8, hop, partner, s_in.at[block], s_in.at[block]) for hop, block in enumerate(senders)]
    )
    near = second_hop(near, row_dp.at[1], row_pr.at[1], 1)
    arrive(near_move + onward)
    for block in range(parts):
        first = (block // 2 + half * (block % 2)) * crop_rows
        at = slice(first, first + crop_rows)
        crops_now = s_in[block, 0:crop_rows, :]
        high, low = split(crops_now)
        s_hi[at, :] = high
        s_lo[at, :] = low
        count = jnp.broadcast_to(s_in[block, count_at:count_at + 1, :], (LANES, width)).T
        counted[at, :] = crops_now * jnp.concatenate([count[0:crop_rows, :]] * (width // LANES), axis=1)
    counted_t[...] = counted[...].T
    mixed_t[...] = s_in[:, mixed_at:count_at, :].reshape(parts * teach_rows, width).T
    scores(0)
    scale = 1.0 / result(near, row_pr.at[1])
    near = first_hop(balance(scale), row_dp.at[2], 6)

    scores(1)
    tot_near = first_hop(fold(lane_part[...].T), tot_dp, 7)
    near = second_hop(near, row_dp.at[2], row_pr.at[2], 2)
    feature_tiles(1 - parity, True)
    tot_near = second_hop(tot_near, tot_dp, tot_pr, 3)
    feature_tiles(parity, False)
    targets = dot3((unit_hi[...], unit_lo[...]), split(assign[...]), NN)
    scale = 1.0 / result(near, row_pr.at[2])
    mixed_pieces = split(mixed_t[...] * scale)
    g_send[...] = (targets * scale).T
    g_moves = start([
        dp_move(11, hop, peer, g_send.at[rows(peer, teach_rows), :], g_dp.at[me])
        for hop, peer in enumerate(dp_peers)
    ])
    g_dp[me] = g_send[rows(me, teach_rows), :]
    f_near = [f_move(step) for step in range(half // 2)]
    arrive(f_near)
    sends.extend(f_near)
    own_half = pl.ds(pl.multiple_of(parity * half_rows, half_rows), half_rows)
    f_send[own_half, :] = f_send[own_half, :] + f_pair[...]
    slot = me // 2
    f_moves = start([
        dp_move(10, hop, peer, f_send.at[rows(place_of(peer), crop_rows), :], f_dp.at[slot])
        for hop, peer in enumerate(twins)
    ])
    f_dp[slot] = f_send[rows(place_of(me), crop_rows), :]
    inverse_row = 1.0 / result(tot_near, tot_pr)
    weighted_t = split(counted_t[...] * inverse_row)
    lane_part[...] = jnp.broadcast_to(inverse_row, (LANES, parts * crop_rows)).T

    chunk = share // CHUNKS
    piece_rows = f_part.shape[0] // groups
    back_moves, home_moves = [], []
    for piece in range(CHUNKS):
        at = slice(piece * chunk, (piece + 1) * chunk)
        grad = coef * (
            dot3(weighted_t, (expo_hi[:, at], expo_lo[:, at]), NN)
            - dot3(mixed_pieces, split(assign[at, :]), NT)
        )
        now = sp_in[:, at]
        inverse = inv_norm[0:1, at]
        unit = now * inverse
        proto_grad = (grad - unit * jnp.sum(unit * grad, axis=0, keepdims=True)) * inverse
        square = jnp.sum(proto_grad * proto_grad, axis=0, keepdims=True) / width
        moved[:, at] = proto_grad * (1.0 / jnp.sqrt(square + square_eps))
        place = pl.ds(pl.multiple_of(me * share + piece * chunk, chunk), chunk)
        back_moves += start([
            dp_move(12 + piece, hop, peer, moved.at[rows(peer, own_rows), at], step_ref.at[:, place])
            for hop, peer in enumerate(dp_peers)
        ])
        home_moves.append(pltpu.make_async_copy(moved.at[own_block, at], step_ref.at[:, place], local_sem.at[2 + piece]))
        home_moves[-1].start()
        if piece == 1:
            arrive(f_moves)
            f_part[0:crop_rows, :] = jnp.sum(f_dp[...], axis=0)
            if f_part.shape[0] > crop_rows:
                f_part[crop_rows:, :] = jnp.zeros((f_part.shape[0] - crop_rows, width), f32)
            f_across = start([
                pr_move(4, hop, peer, f_part.at[rows(peer, piece_rows), :], f_pr.at[mine])
                for hop, peer in enumerate(pr_peers)
            ])
            f_pr[mine] = f_part[rows(mine, piece_rows), :]
    arrive(f_across)
    own_piece = rows(mine, piece_rows)
    f_sum[own_piece, :] = jnp.sum(f_pr[...], axis=0)
    f_last = start(
        [pr_move(6, hop, peer, f_sum.at[own_piece, :], f_sum.at[own_piece, :]) for hop, peer in enumerate(pr_peers)]
    )
    arrive(g_moves)
    g_pr[mine] = jnp.sum(g_dp[...], axis=0)
    g_across = start(
        [pr_move(5, hop, peer, g_pr.at[mine], g_pr.at[mine]) for hop, peer in enumerate(pr_peers)]
    )
    teach = lax.broadcasted_iota(jnp.int32, (crop_rows, teach_rows), 1)
    same = crops_ref[:, 0:1] == teach // GLOBAL_CROPS
    other = crops_ref[:, 1:2] != teach % GLOBAL_CROPS
    pairs = jnp.where(same & other, 1.0, 0.0).astype(f32)
    count = jnp.sum(pairs, axis=1, keepdims=True)
    inverse = jnp.concatenate([lane_part[rows(place_of(me), crop_rows), :]] * (width // LANES), axis=1)
    s_values = sf_ref[...]
    s_norm = jnp.sqrt(jnp.sum(s_values * s_values, axis=1, keepdims=True) + norm_eps)
    s_unit = s_values / s_norm
    arrive(g_across)
    wanted = dot(pairs, jnp.sum(g_pr[...], axis=0), NN)
    arrive(f_last)
    feature_unit = coef * (count * (f_sum[0:crop_rows, :] * inverse) - wanted)
    fgrad_ref[...] = (
        feature_unit - s_unit * jnp.sum(s_unit * feature_unit, axis=1, keepdims=True)
    ) / s_norm
    arrive(back_moves)
    for move in home_moves:
        move.wait()
    for move in sends:
        move.wait_send()


def body(student_feats, teacher_feats, student_proto, teacher_proto, crops, step):
    parts, groups = lax.axis_size("dp"), lax.axis_size("proto")
    crop_rows, width = student_feats.shape
    teach_rows = teacher_feats.shape[0]
    own_rows, columns = student_proto.shape
    share = columns // parts
    images = teach_rows // GLOBAL_CROPS * parts
    pair_total = GLOBAL_CROPS * (GLOBAL_CROPS - 1) + (CROPS - GLOBAL_CROPS) * GLOBAL_CROPS
    coef = loss_scale / (pair_total * images * student_temp)
    all_s, all_t = parts * crop_rows, parts * teach_rows
    packed = crop_rows + teach_rows + SUBLANES
    kinds = 13 + CHUNKS
    piece_rows = -(-crop_rows // (groups * SUBLANES)) * SUBLANES
    rate, teacher_temp, momentum = plan(step)

    def vmem(*shape, dtype=f32):
        return pltpu.VMEM(shape, dtype)

    def sems(*shape):
        return pltpu.SemaphoreType.DMA(shape)

    whole, outside = pl.BlockSpec(memory_space=pltpu.VMEM), pl.BlockSpec(memory_space=pl.ANY)
    shapes = [student_proto, student_feats]
    direction, feature_grad = pl.pallas_call(
        functools.partial(kernel, parts, groups, coef),
        out_shape=[jax.ShapeDtypeStruct(one.shape, f32) for one in shapes],
        in_specs=[pl.BlockSpec(memory_space=pltpu.SMEM), whole, whole, outside, outside, whole],
        out_specs=[outside, whole],
        scratch_shapes=[
            vmem(width, share), vmem(width, share),
            vmem(parts, packed, width), vmem(all_t, width),
            vmem(packed, width), vmem(teach_rows, width),
            vmem(width, share, dtype=bf16), vmem(width, share, dtype=bf16),
            vmem(all_s, share, dtype=bf16), vmem(all_s, share, dtype=bf16),
            vmem(all_s, width, dtype=bf16), vmem(all_s, width, dtype=bf16),
            vmem(all_s, LANES), vmem(all_s, width), vmem(width, all_s), vmem(width, all_t),
            vmem(share, all_t),
            vmem(ITERS, parts, 1, all_t), vmem(ITERS, groups, 1, all_t),
            vmem(parts, 1, all_s), vmem(groups, 1, all_s),
            vmem(-(-crop_rows // LANES) * LANES, -(-teach_rows // LANES) * LANES),
            vmem(SUBLANES, share), vmem(all_s, width), vmem(all_s // 2, width),
            vmem(parts // 2, crop_rows, width), vmem(groups * piece_rows, width),
            vmem(groups, piece_rows, width), vmem(groups * piece_rows, width),
            vmem(all_t, width), vmem(parts, teach_rows, width), vmem(groups, teach_rows, width),
            vmem(width, share),
            sems(kinds, parts), sems(kinds, parts), sems(7, groups), sems(7, groups), sems(2 + CHUNKS),
        ],
        compiler_params=pltpu.CompilerParams(
            collective_id=0, has_side_effects=True, vmem_limit_bytes=56 * 1024 * 1024
        ),
    )(step, student_feats, teacher_feats, student_proto, teacher_proto, crops)
    student_next = student_proto - rate * (direction + weight_decay * student_proto)
    teacher_next = momentum * teacher_proto + (1.0 - momentum) * student_next
    return (student_next, teacher_next, feature_grad)


def solution(mesh):
    in_specs = (
        P("dp", None),
        P("dp", None),
        P("dp", "proto"),
        P("dp", "proto"),
        P("dp", None),
        P(),
    )
    out_specs = (P("dp", "proto"), P("dp", "proto"), P("dp", None))
    return jax.shard_map(body, mesh=mesh, in_specs=in_specs, out_specs=out_specs, check_vma=False)
```

```python
import functools

import jax
import jax.numpy as jnp
from jax import lax
from jax.experimental import pallas as pl
from jax.experimental.pallas import tpu as pltpu
from jax.sharding import PartitionSpec as P

CROPS = 10
GLOBAL_CROPS = 2
ITERS = 3
WARM_STEPS = 12500
TOTAL_STEPS = 625000


student_temp = 0.1
loss_scale = 16777216.0
norm_eps = 1e-06
square_eps = 1e-06
rate_peak = 0.05
weight_decay = 0.04
momentum_base = 0.994
highest = lax.Precision.HIGHEST


def plan(step):
    value = step[0].astype(jnp.float32)
    ramp = jnp.minimum(1.0, value / WARM_STEPS)
    rate = rate_peak * (0.25 + 0.75 * ramp)
    teacher_temp = 0.04 + 0.03 * ramp
    momentum = 1.0 - (1.0 - momentum_base) * (jnp.cos(jnp.pi * value / TOTAL_STEPS) + 1.0) * 0.5
    return (rate, teacher_temp, momentum)


NN = (((1,), (0,)), ((), ()))
NT = (((1,), (1,)), ((), ()))
MESH = pl.DeviceIdType.MESH
LANES = 128
SUBLANES = 8
CHUNKS = 4
f32 = jnp.float32
bf16 = jnp.bfloat16


def dot(left, right, dims):
    return lax.dot_general(left, right, dims, precision=highest, preferred_element_type=f32)


def split(values):
    high = values.astype(bf16)
    return high, (values - high.astype(f32)).astype(bf16)


def dot3(left, right, dims):
    def one(a, b):
        return lax.dot_general(a, b, dims, preferred_element_type=f32)

    return one(left[0], right[0]) + (one(left[0], right[1]) + one(left[1], right[0]))


def fold(values):
    return jnp.sum(values, axis=0, keepdims=True)


def kernel(
    parts, groups, coef,
    plan_ref, sf_ref, tf_ref, sp_ref, tp_ref, crops_ref,
    step_ref, fgrad_ref,
    sp_in, tp_in, s_in, t_in, own_s, own_t, unit_hi, unit_lo, expo_hi, expo_lo,
    s_hi, s_lo, lane_part, counted, counted_t, mixed_t, assign, row_dp, row_pr, tot_dp, tot_pr,
    pair_pad, inv_norm, f_send, f_pair, f_dp, f_part, f_pr, f_sum, g_send, g_dp, g_pr, moved,
    dp_send, dp_recv, pr_send, pr_recv, local_sem,
):
    me, mine = lax.axis_index("dp"), lax.axis_index("proto")
    crop_rows, width = sf_ref.shape
    teach_rows = tf_ref.shape[0]
    own_rows, columns = sp_ref.shape
    share = columns // parts
    half = parts // 2
    temp = 0.04 + 0.03 * jnp.minimum(1.0, plan_ref[0].astype(f32) / WARM_STEPS)
    parity = lax.rem(me, 2)
    partner = me + 1 - 2 * parity
    twins = [lax.rem(me + 2 * hop, parts) for hop in range(1, half)]
    senders = [lax.rem(me + parts - 2 * hop, parts) for hop in range(1, half)]
    dp_peers = [lax.rem(me + hop, parts) for hop in range(1, parts)]
    pr_peers = [lax.rem(mine + hop, groups) for hop in range(1, groups)]
    barrier = pltpu.get_barrier_semaphore()
    for peer in dp_peers:
        pl.semaphore_signal(barrier, inc=1, device_id={"dp": peer}, device_id_type=MESH)
    for peer in pr_peers:
        pl.semaphore_signal(barrier, inc=1, device_id={"proto": peer}, device_id_type=MESH)
    sends = []

    def cols(which):
        return pl.ds(pl.multiple_of(which * share, share), share)

    def rows(which, size):
        return pl.ds(pl.multiple_of(which * size, size), size)

    def dp_move(kind, hop, peer, src, dst):
        return pltpu.make_async_remote_copy(
            src_ref=src, dst_ref=dst, send_sem=dp_send.at[kind, hop], recv_sem=dp_recv.at[kind, hop],
            device_id={"dp": peer}, device_id_type=MESH,
        )

    def pr_move(kind, hop, peer, src, dst):
        return pltpu.make_async_remote_copy(
            src_ref=src, dst_ref=dst, send_sem=pr_send.at[kind, hop], recv_sem=pr_recv.at[kind, hop],
            device_id={"proto": peer}, device_id_type=MESH,
        )

    def start(moves):
        for move in moves:
            move.start()
            sends.append(move)
        return moves

    def arrive(moves):
        for move in moves:
            move.wait_recv()

    own_block = rows(me, own_rows)
    local_moves = [
        pltpu.make_async_copy(tp_ref.at[:, cols(me)], tp_in.at[own_block, :], local_sem.at[0]),
        pltpu.make_async_copy(sp_ref.at[:, cols(me)], sp_in.at[own_block, :], local_sem.at[1]),
    ]
    for move in local_moves:
        move.start()
    t_values = tf_ref[...]
    own_t[...] = t_values / jnp.sqrt(jnp.sum(t_values * t_values, axis=1, keepdims=True) + norm_eps)
    pl.semaphore_wait(barrier, parts - 1 + groups - 1)

    teacher_moves = start(
        [dp_move(0, hop, peer, tp_ref.at[:, cols(peer)], tp_in.at[own_block, :]) for hop, peer in enumerate(dp_peers)]
        + [dp_move(1, hop, peer, own_t, t_in.at[rows(me, teach_rows), :]) for hop, peer in enumerate(dp_peers)]
    )
    t_in[rows(me, teach_rows), :] = own_t[...]

    s_values = sf_ref[...]
    s_norm = jnp.sqrt(jnp.sum(s_values * s_values, axis=1, keepdims=True) + norm_eps)
    s_unit = s_values / s_norm
    teach = lax.broadcasted_iota(jnp.int32, (crop_rows, pair_pad.shape[1]), 1)
    same = crops_ref[:, 0:1] == teach // GLOBAL_CROPS
    other = crops_ref[:, 1:2] != teach % GLOBAL_CROPS
    pair_pad[...] = jnp.zeros(pair_pad.shape, f32)
    pair_pad[0:crop_rows, :] = jnp.where(same & other & (teach < teach_rows), 1.0, 0.0).astype(f32)
    pairs_t = pair_pad[...].T[0:teach_rows, 0:crop_rows]
    mixed_at, count_at = crop_rows, crop_rows + teach_rows
    own_s[0:crop_rows, :] = s_unit
    own_s[mixed_at:count_at, :] = dot(pairs_t, s_unit, NN)
    own_s[count_at:, :] = jnp.zeros((SUBLANES, width), f32)
    own_s[count_at:, 0:crop_rows] = jnp.broadcast_to(
        jnp.sum(pairs_t, axis=0, keepdims=True), (SUBLANES, crop_rows)
    )
    s_in[me] = own_s[...]
    for move in local_moves:
        move.wait()

    def first_hop(values, first, kind):
        first[me] = values
        return start(
            [dp_move(kind, hop, peer, first.at[me], first.at[me]) for hop, peer in enumerate(dp_peers)]
        )

    def second_hop(moves, first, second, kind):
        arrive(moves)
        second[mine] = jnp.sum(first[...], axis=0)
        return start(
            [pr_move(kind, hop, peer, second.at[mine], second.at[mine]) for hop, peer in enumerate(pr_peers)]
        )

    def result(moves, second):
        arrive(moves)
        return jnp.sum(second[...], axis=0)

    def balance(scale):
        values = assign[...]
        if scale is not None:
            values = values * scale
        values = values * (1.0 / jnp.sum(values, axis=1, keepdims=True))
        assign[...] = values
        return fold(values)

    tile = 2 * crop_rows
    half_rows = half * crop_rows

    def place_of(block):
        return (block // 2) + half * lax.rem(block, 2)

    def scores(side):
        at_cols = slice(side * wide, (side + 1) * wide)
        arrive(proto_moves[side])
        now = sp_in[:, at_cols]
        inverse = 1.0 / jnp.sqrt(jnp.sum(now * now, axis=0, keepdims=True) + norm_eps)
        inv_norm[:, at_cols] = jnp.broadcast_to(inverse, (SUBLANES, wide))
        high, low = split(now * inverse)
        unit_hi[:, at_cols] = high
        unit_lo[:, at_cols] = low

        def score_tile(step, carry):
            at = rows(step, tile)
            unit = (unit_hi[:, at_cols], unit_lo[:, at_cols])
            expo = jnp.exp(dot3((s_hi[at, :], s_lo[at, :]), unit, NN) * (1.0 / student_temp))
            part = expo[:, 0:LANES]
            for lane in range(1, wide // LANES):
                part = part + expo[:, lane * LANES:(lane + 1) * LANES]
            lane_part[at, :] = part if side == 0 else lane_part[at, :] + part
            pieces = split(expo)
            expo_hi[at, at_cols] = pieces[0]
            expo_lo[at, at_cols] = pieces[1]
            return carry

        lax.fori_loop(0, half, score_tile, 0)

    def f_move(step):
        at = pl.ds(pl.multiple_of((1 - parity) * half_rows + step * tile, tile), tile)
        return dp_move(9, step, partner, f_send.at[at, :], f_pair.at[rows(step, tile), :])

    def feature_tiles(which, near):
        def feature_tile(step, carry):
            at = pl.ds(pl.multiple_of(which * half_rows + step * tile, tile), tile)
            f_send[at, :] = dot3((expo_hi[at, :], expo_lo[at, :]), (unit_hi[...], unit_lo[...]), NT)
            if near:
                f_move(step).start()
            return carry

        lax.fori_loop(0, half // 2, feature_tile, 0)

    arrive(teacher_moves)
    teacher_cols = tp_in[...]
    inverse = 1.0 / jnp.sqrt(jnp.sum(teacher_cols * teacher_cols, axis=0, keepdims=True) + norm_eps)
    assign[...] = jnp.exp(dot((teacher_cols * inverse).T, t_in[...], NT) * (1.0 / temp))
    near = first_hop(balance(None), row_dp.at[0], 4)
    near_move = start([dp_move(3, 0, partner, own_s, s_in.at[me])])
    twin_moves = start([dp_move(3, hop + 1, peer, own_s, s_in.at[me]) for hop, peer in enumerate(twins)])
    near = second_hop(near, row_dp.at[0], row_pr.at[0], 0)
    scale = 1.0 / result(near, row_pr.at[0])
    near = first_hop(balance(scale), row_dp.at[1], 5)
    wide = share // 2
    proto_moves = []
    for side in range(2):
        proto_moves.append(start([
            dp_move(
                (2, 12 + CHUNKS)[side], hop, peer,
                sp_ref.at[:, pl.ds(pl.multiple_of(peer * share + side * wide, wide), wide)],
                sp_in.at[own_block, side * wide:(side + 1) * wide],
            )
            for hop, peer in enumerate(dp_peers)
        ]))
    arrive(twin_moves)
    onward = start(
        [dp_move(8, hop, partner, s_in.at[block], s_in.at[block]) for hop, block in enumerate(senders)]
    )
    near = second_hop(near, row_dp.at[1], row_pr.at[1], 1)
    arrive(near_move + onward)
    for block in range(parts):
        first = (block // 2 + half * (block % 2)) * crop_rows
        at = slice(first, first + crop_rows)
        crops_now = s_in[block, 0:crop_rows, :]
        high, low = split(crops_now)
        s_hi[at, :] = high
        s_lo[at, :] = low
        count = jnp.broadcast_to(s_in[block, count_at:count_at + 1, :], (LANES, width)).T
        counted[at, :] = crops_now * jnp.concatenate([count[0:crop_rows, :]] * (width // LANES), axis=1)
    counted_t[...] = counted[...].T
    mixed_t[...] = s_in[:, mixed_at:count_at, :].reshape(parts * teach_rows, width).T
    scores(0)
    scale = 1.0 / result(near, row_pr.at[1])
    near = first_hop(balance(scale), row_dp.at[2], 6)

    scores(1)
    tot_near = first_hop(fold(lane_part[...].T), tot_dp, 7)
    near = second_hop(near, row_dp.at[2], row_pr.at[2], 2)
    feature_tiles(1 - parity, True)
    tot_near = second_hop(tot_near, tot_dp, tot_pr, 3)
    feature_tiles(parity, False)
    f_near = [f_move(step) for step in range(half // 2)]
    arrive(f_near)
    sends.extend(f_near)
    own_half = pl.ds(pl.multiple_of(parity * half_rows, half_rows), half_rows)
    f_send[own_half, :] = f_send[own_half, :] + f_pair[...]
    slot = me // 2
    f_moves = start([
        dp_move(10, hop, peer, f_send.at[rows(place_of(peer), crop_rows), :], f_dp.at[slot])
        for hop, peer in enumerate(twins)
    ])
    f_dp[slot] = f_send[rows(place_of(me), crop_rows), :]
    targets = dot3((unit_hi[...], unit_lo[...]), split(assign[...]), NN)
    scale = 1.0 / result(near, row_pr.at[2])
    mixed_pieces = split(mixed_t[...] * scale)
    g_send[...] = (targets * scale).T
    g_moves = start([
        dp_move(11, hop, peer, g_send.at[rows(peer, teach_rows), :], g_dp.at[me])
        for hop, peer in enumerate(dp_peers)
    ])
    g_dp[me] = g_send[rows(me, teach_rows), :]
    inverse_row = 1.0 / result(tot_near, tot_pr)
    weighted_t = split(counted_t[...] * inverse_row)
    lane_part[...] = jnp.broadcast_to(inverse_row, (LANES, parts * crop_rows)).T

    chunk = share // CHUNKS
    piece_rows = f_part.shape[0] // groups
    back_moves, home_moves = [], []
    for piece in range(CHUNKS):
        at = slice(piece * chunk, (piece + 1) * chunk)
        grad = coef * (
            dot3(weighted_t, (expo_hi[:, at], expo_lo[:, at]), NN)
            - dot3(mixed_pieces, split(assign[at, :]), NT)
        )
        now = sp_in[:, at]
        inverse = inv_norm[0:1, at]
        unit = now * inverse
        proto_grad = (grad - unit * jnp.sum(unit * grad, axis=0, keepdims=True)) * inverse
        square = jnp.sum(proto_grad * proto_grad, axis=0, keepdims=True) / width
        moved[:, at] = proto_grad * (1.0 / jnp.sqrt(square + square_eps))
        place = pl.ds(pl.multiple_of(me * share + piece * chunk, chunk), chunk)
        back_moves += start([
            dp_move(12 + piece, hop, peer, moved.at[rows(peer, own_rows), at], step_ref.at[:, place])
            for hop, peer in enumerate(dp_peers)
        ])
        home_moves.append(pltpu.make_async_copy(moved.at[own_block, at], step_ref.at[:, place], local_sem.at[2 + piece]))
        home_moves[-1].start()
        if piece == 1:
            arrive(f_moves)
            f_part[0:crop_rows, :] = jnp.sum(f_dp[...], axis=0)
            if f_part.shape[0] > crop_rows:
                f_part[crop_rows:, :] = jnp.zeros((f_part.shape[0] - crop_rows, width), f32)
            f_across = start([
                pr_move(4, hop, peer, f_part.at[rows(peer, piece_rows), :], f_pr.at[mine])
                for hop, peer in enumerate(pr_peers)
            ])
            f_pr[mine] = f_part[rows(mine, piece_rows), :]
    arrive(f_across)
    own_piece = rows(mine, piece_rows)
    f_sum[own_piece, :] = jnp.sum(f_pr[...], axis=0)
    f_last = start(
        [pr_move(6, hop, peer, f_sum.at[own_piece, :], f_sum.at[own_piece, :]) for hop, peer in enumerate(pr_peers)]
    )
    arrive(g_moves)
    g_pr[mine] = jnp.sum(g_dp[...], axis=0)
    g_across = start(
        [pr_move(5, hop, peer, g_pr.at[mine], g_pr.at[mine]) for hop, peer in enumerate(pr_peers)]
    )
    teach = lax.broadcasted_iota(jnp.int32, (crop_rows, teach_rows), 1)
    same = crops_ref[:, 0:1] == teach // GLOBAL_CROPS
    other = crops_ref[:, 1:2] != teach % GLOBAL_CROPS
    pairs = jnp.where(same & other, 1.0, 0.0).astype(f32)
    count = jnp.sum(pairs, axis=1, keepdims=True)
    inverse = jnp.concatenate([lane_part[rows(place_of(me), crop_rows), :]] * (width // LANES), axis=1)
    s_values = sf_ref[...]
    s_norm = jnp.sqrt(jnp.sum(s_values * s_values, axis=1, keepdims=True) + norm_eps)
    s_unit = s_values / s_norm
    arrive(g_across)
    wanted = dot(pairs, jnp.sum(g_pr[...], axis=0), NN)
    arrive(f_last)
    feature_unit = coef * (count * (f_sum[0:crop_rows, :] * inverse) - wanted)
    fgrad_ref[...] = (
        feature_unit - s_unit * jnp.sum(s_unit * feature_unit, axis=1, keepdims=True)
    ) / s_norm
    arrive(back_moves)
    for move in home_moves:
        move.wait()
    for move in sends:
        move.wait_send()


def body(student_feats, teacher_feats, student_proto, teacher_proto, crops, step):
    parts, groups = lax.axis_size("dp"), lax.axis_size("proto")
    crop_rows, width = student_feats.shape
    teach_rows = teacher_feats.shape[0]
    own_rows, columns = student_proto.shape
    share = columns // parts
    images = teach_rows // GLOBAL_CROPS * parts
    pair_total = GLOBAL_CROPS * (GLOBAL_CROPS - 1) + (CROPS - GLOBAL_CROPS) * GLOBAL_CROPS
    coef = loss_scale / (pair_total * images * student_temp)
    all_s, all_t = parts * crop_rows, parts * teach_rows
    packed = crop_rows + teach_rows + SUBLANES
    kinds = 13 + CHUNKS
    piece_rows = -(-crop_rows // (groups * SUBLANES)) * SUBLANES
    rate, teacher_temp, momentum = plan(step)

    def vmem(*shape, dtype=f32):
        return pltpu.VMEM(shape, dtype)

    def sems(*shape):
        return pltpu.SemaphoreType.DMA(shape)

    whole, outside = pl.BlockSpec(memory_space=pltpu.VMEM), pl.BlockSpec(memory_space=pl.ANY)
    shapes = [student_proto, student_feats]
    direction, feature_grad = pl.pallas_call(
        functools.partial(kernel, parts, groups, coef),
        out_shape=[jax.ShapeDtypeStruct(one.shape, f32) for one in shapes],
        in_specs=[pl.BlockSpec(memory_space=pltpu.SMEM), whole, whole, outside, outside, whole],
        out_specs=[outside, whole],
        scratch_shapes=[
            vmem(width, share), vmem(width, share),
            vmem(parts, packed, width), vmem(all_t, width),
            vmem(packed, width), vmem(teach_rows, width),
            vmem(width, share, dtype=bf16), vmem(width, share, dtype=bf16),
            vmem(all_s, share, dtype=bf16), vmem(all_s, share, dtype=bf16),
            vmem(all_s, width, dtype=bf16), vmem(all_s, width, dtype=bf16),
            vmem(all_s, LANES), vmem(all_s, width), vmem(width, all_s), vmem(width, all_t),
            vmem(share, all_t),
            vmem(ITERS, parts, 1, all_t), vmem(ITERS, groups, 1, all_t),
            vmem(parts, 1, all_s), vmem(groups, 1, all_s),
            vmem(-(-crop_rows // LANES) * LANES, -(-teach_rows // LANES) * LANES),
            vmem(SUBLANES, share), vmem(all_s, width), vmem(all_s // 2, width),
            vmem(parts // 2, crop_rows, width), vmem(groups * piece_rows, width),
            vmem(groups, piece_rows, width), vmem(groups * piece_rows, width),
            vmem(all_t, width), vmem(parts, teach_rows, width), vmem(groups, teach_rows, width),
            vmem(width, share),
            sems(kinds, parts), sems(kinds, parts), sems(7, groups), sems(7, groups), sems(2 + CHUNKS),
        ],
        compiler_params=pltpu.CompilerParams(
            collective_id=0, has_side_effects=True, vmem_limit_bytes=56 * 1024 * 1024
        ),
    )(step, student_feats, teacher_feats, student_proto, teacher_proto, crops)
    student_next = student_proto - rate * (direction + weight_decay * student_proto)
    teacher_next = momentum * teacher_proto + (1.0 - momentum) * student_next
    return (student_next, teacher_next, feature_grad)


def solution(mesh):
    in_specs = (
        P("dp", None),
        P("dp", None),
        P("dp", "proto"),
        P("dp", "proto"),
        P("dp", None),
        P(),
    )
    out_specs = (P("dp", "proto"), P("dp", "proto"), P("dp", None))
    return jax.shard_map(body, mesh=mesh, in_specs=in_specs, out_specs=out_specs, check_vma=False)
```
